512 devices in a mesh: ctx: 32 (over x, y), tp: 16 (over z, core).
Axes of the slice: x: 4, y: 8, z: 8, core: 2. Of those that a mesh axis runs over, the one named last changes fastest.
Arguments:
- queries: bfloat16 [2, 512, 4096], P(None, 'ctx', 'tp'), may hold values from -20 to 20
- positions: int32 [2, 512], P(None, 'ctx'), may hold values from 0 to 32767, as said below
- cached_keys: bfloat16 [2, 32768, 4096], P(None, 'ctx', 'tp'), may hold values from -64 to 64
- cached_values: bfloat16 [2, 32768, 4096], P(None, 'ctx', 'tp'), may hold values from -24 to 24
- residual_rows: bfloat16 [2, 512, 4096], P(None, 'ctx', 'tp'), may hold values from -150 to 150
- out_proj: bfloat16 [4096, 4096], P('tp', 'ctx'), may hold values from -0.09375 to 0.09375
- norm_gain: bfloat16 [4096], P('tp'), may hold values from 0.5 to 1.5
- head_weight: bfloat16 [4096, 65536], P(None, ('ctx', 'tp')), may hold values from -1 to 1
- targets: int32 [2, 512], P(None, 'ctx'), may hold values from 0 to 65535
- live_rows: int32 [2], replicated, may hold values from 128 to 512, as said below
- mask_total: int32 [2], replicated, may hold values from 512 to 2048
Outputs:
- token_nll: float32 [2, 512], P(None, 'ctx')
- elbo_estimate: float32 [], replicated
The draws below stay inside these ranges and needn't reach their ends.
Inputs may be any that keep to these rules, and one draw needn't show every extreme that they name: Within a sample the positions are distinct. One of the samples has all 512 slots live; slots below live_rows hold masked tokens.
All inputs are finite; a program needn't handle non-finite values.
Results may differ from the reference program's by a relative error of at most 0.001.
Values may be sent and summed in bfloat16 or wider, within the bound.
A program may use at most 64 MiB of HBM per device.

```python
import math
import jax
import jax.numpy as jnp
from jax import lax

D = 4096
HEADS = 32
HEAD_SIZE = 128
VOCAB = 65536
SAMPLES = 2
L = 32768
M = 512


def common_parts(key):
    queries_f = 2.5 * jax.random.normal(jax.random.fold_in(key, 11), (SAMPLES, M, D), jnp.float32)
    queries_f = jnp.clip(queries_f, -19.0, 19.0)
    spot_rows = [jax.random.permutation(jax.random.fold_in(key, 12 + sample_id), L)[:M] for sample_id in range(SAMPLES)]
    spot_table = jnp.stack(spot_rows).astype(jnp.int32)
    return (queries_f, spot_table)


def draw_queries(key, part):
    queries_f, spot_table = common_parts(key)
    return queries_f.astype(jnp.bfloat16)


def draw_positions(key, part):
    queries_f, spot_table = common_parts(key)
    return spot_table


def draw_cached_keys(key, part):
    key = jax.random.fold_in(key, 21)
    keys_f = jax.random.normal(key, (SAMPLES, L, D), jnp.float32)
    return jnp.clip(keys_f, -63.0, 63.0).astype(jnp.bfloat16)


def draw_residual_rows(key, part):
    key = jax.random.fold_in(key, 31)
    base_key, row_key, column_key = jax.random.split(key, 3)
    column_scale = jnp.exp(jax.random.uniform(column_key, (D,), jnp.float32, math.log(0.5), math.log(1.5)))
    column_scale = column_scale * 3.0 ** (jnp.arange(D, dtype=jnp.float32) / D)
    row_scale = jnp.exp(jax.random.uniform(row_key, (SAMPLES, M, 1), jnp.float32, math.log(0.3), math.log(3.0)))
    resid_f = jax.random.normal(base_key, (SAMPLES, M, D), jnp.float32) * row_scale * column_scale
    return jnp.clip(resid_f, -149.0, 149.0).astype(jnp.bfloat16)


def draw_head_weight(key, part):
    key = jax.random.fold_in(key, 41)
    scale = 3.0 / math.sqrt(D)
    weight_f = scale * jax.random.normal(key, (D, VOCAB), jnp.float32)
    return jnp.clip(weight_f, -0.99, 0.99).astype(jnp.bfloat16)


def draw_live_rows(key, part):
    key = jax.random.fold_in(key, 51)
    count_key, chosen_key = jax.random.split(key)
    counts = jax.random.randint(count_key, (SAMPLES,), M // 4, M + 1)
    chosen = jax.random.randint(chosen_key, (), 0, SAMPLES)
    return counts.at[chosen].set(M).astype(jnp.int32)


def set_ends(array, key, smallest, high):
    shape = array.shape
    place = [jax.random.randint(jax.random.fold_in(key, axis), (), 0, shape[axis]) for axis in range(len(shape))]
    array = array.at[tuple(place)].set(smallest)
    longest = shape.index(max(shape))
    place[longest] = (place[longest] + 1) % shape[longest]
    return array.at[tuple(place)].set(high)


def block_levels(own_key, dims, pieces, smallest, top_value):
    loudness, own = 1.0, jax.random.fold_in(own_key, 6)
    for axis_at, blocks in pieces:
        heights = jnp.exp(jax.random.uniform(jax.random.fold_in(own, axis_at), (blocks,), jnp.float32, smallest / len(pieces), top_value / len(pieces)))
        loudness = loudness * jnp.repeat(heights, dims[axis_at] // blocks).reshape([-1 if axis == axis_at else 1 for axis in range(len(dims))])
    return loudness


def normal_values(rng, dims, deviation, most, pieces=(), held_as=jnp.bfloat16):
    values = jax.random.normal(rng, dims, jnp.float32) * deviation
    if len(pieces) > 0:
        values = block_levels(rng, dims, pieces, -0.22, 0.18) * values
    return jnp.clip(values, min=-most, max=most).astype(held_as)


def setup_inputs(seed: int = 0) -> dict:
    key_list = jax.random.split(jax.random.key(seed), 12)
    return {
        "queries": draw_queries(jax.random.fold_in(key_list[11], 71), 0),
        "positions": draw_positions(jax.random.fold_in(key_list[11], 71), 0),
        "cached_keys": draw_cached_keys(jax.random.fold_in(key_list[11], 71), 0),
        "cached_values": normal_values(key_list[3], (SAMPLES, L, D), 4.0, 24.0, ((1, 32), (2, 16))),
        "residual_rows": draw_residual_rows(jax.random.fold_in(key_list[11], 71), 0),
        "out_proj": normal_values(key_list[5], (D, D), D ** -0.5, 0.09375, ((0, 16), (1, 32))),
        "norm_gain": jnp.clip(1.0 + 0.1 * jax.random.normal(key_list[6], (D,), jnp.float32), 0.5, 1.5).astype(jnp.bfloat16),
        "head_weight": draw_head_weight(jax.random.fold_in(key_list[11], 71), 0),
        "targets": set_ends(jax.random.randint(key_list[8], (SAMPLES, M), 0, VOCAB), jax.random.fold_in(key_list[8], 1), 0, VOCAB - 1).astype(jnp.int32),
        "live_rows": draw_live_rows(jax.random.fold_in(key_list[11], 71), 0),
        "mask_total": jax.random.randint(key_list[10], (SAMPLES,), M, 4 * M + 1).astype(jnp.int32),
    }


ROPE_BASE = 500000.0
NORM_EPSILON = 1e-05

def rotate(query_block, spot_table):
    halfway = query_block.shape[-1] // 2
    frequency = ROPE_BASE ** (-2.0 * jnp.arange(halfway, dtype=jnp.float32) / query_block.shape[-1])
    angles = spot_table.astype(jnp.float32)[..., None, None] * frequency
    cosine = jnp.cos(angles)
    sine_part = jnp.sin(angles)
    leading = query_block[..., :halfway]
    trailing = query_block[..., halfway:]
    return jnp.concatenate([leading * cosine - trailing * sine_part, trailing * cosine + leading * sine_part], -1)

def reference(queries, positions, cached_keys, cached_values, residual_rows, out_proj, norm_gain, head_weight, targets, live_rows, mask_total):
    rotated = rotate(queries.astype(jnp.float32).reshape(SAMPLES, M, HEADS, HEAD_SIZE), positions).astype(jnp.bfloat16)
    stacked = (jnp.moveaxis(rotated, 2, 0), jnp.moveaxis(cached_keys.reshape(SAMPLES, L, HEADS, HEAD_SIZE), 2, 0), jnp.moveaxis(cached_values.reshape(SAMPLES, L, HEADS, HEAD_SIZE), 2, 0))

    def one_head(operands):
        query_slice_local, key_slice_local, value_slice_local = operands
        attention_logits = jnp.einsum('ibj,igj->ibg', query_slice_local.astype(jnp.float32), key_slice_local.astype(jnp.float32)) * (1.0 / math.sqrt(HEAD_SIZE))
        row_top = lax.optimization_barrier(jnp.max(attention_logits, -1, keepdims=True))
        weights = jnp.exp(attention_logits - row_top)
        totals = lax.optimization_barrier(jnp.sum(weights, -1, keepdims=True))
        rounded_values = lax.optimization_barrier(weights.astype(jnp.bfloat16)).astype(jnp.float32)
        softmax_numerator = jnp.einsum('xip,xpn->xin', rounded_values, value_slice_local.astype(jnp.float32))
        return (softmax_numerator / totals).astype(jnp.bfloat16)
    heads_out = lax.map(one_head, stacked)
    attended = jnp.moveaxis(heads_out, 0, 2).reshape(SAMPLES * M, D)
    branch = jnp.dot(attended, out_proj, preferred_element_type=jnp.float32)
    stream = residual_rows.reshape(SAMPLES * M, D).astype(jnp.float32) + branch
    mean_square = lax.optimization_barrier(jnp.mean(stream * stream, -1, keepdims=True))
    normed = (stream * lax.rsqrt(mean_square + NORM_EPSILON) * norm_gain.astype(jnp.float32)).astype(jnp.bfloat16)
    logits = jnp.dot(normed, head_weight, preferred_element_type=jnp.float32).reshape(SAMPLES, M, VOCAB)
    global_peak = lax.optimization_barrier(jnp.max(logits, -1))
    exp_sum = lax.optimization_barrier(jnp.sum(jnp.exp(logits - global_peak[..., None]), -1))
    target_logit = jnp.take_along_axis(logits, targets[..., None].astype(jnp.int32), -1)[..., 0]
    alive_slots = jnp.arange(M, dtype=jnp.int32)[None, :] < live_rows[:, None]
    token_nll = jnp.where(alive_slots, global_peak + jnp.log(exp_sum) - target_logit, jnp.float32(0.0))
    elbo_estimate = jnp.sum(lax.optimization_barrier(jnp.sum(token_nll, 1)) / mask_total.astype(jnp.float32)) / SAMPLES
    return (token_nll, elbo_estimate)
```

```python
import functools
import math

import jax
import jax.numpy as jnp
from jax import lax
from jax.experimental import pallas as pl
from jax.experimental.pallas import tpu as pltpu
from jax.sharding import PartitionSpec as P

HEAD_SIZE = 128
ROPE_BASE = 500000.0
NORM_EPSILON = 1e-05
F32 = jnp.float32
BF16 = jnp.bfloat16


def near_first(n):
    return sorted(range(1, n), key=lambda d: (min(d, n - d), d))


def transposed(tiles):
    stacked = jnp.concatenate(tiles, axis=0)
    if stacked.shape[0] < 128:
        stacked = jnp.concatenate(
            [stacked, jnp.zeros((128 - stacked.shape[0], 128), F32)], axis=0
        )
    return stacked.T


def columns_to_tile(columns):
    rows = columns[0].shape[0]
    lane = lax.broadcasted_iota(jnp.int32, (rows, 128), 1)
    table = jnp.zeros((rows, 128), F32)
    for at, column in enumerate(columns):
        table = jnp.where(lane == at, column, table)
    if rows < 128:
        table = jnp.concatenate([table, jnp.zeros((128 - rows, 128), F32)], axis=0)
    return table.T[:8]


def merge(tiles):
    top = functools.reduce(jnp.maximum, tiles)
    weights = [jnp.exp(tile - top) for tile in tiles]
    total = functools.reduce(jnp.add, weights)
    return [weight / total for weight in weights], top + jnp.log(total)


def kernel(
    sizes,
    q, cosine, sine, target, resid, gain, keys_hbm, values_hbm, proj_hbm, head_hbm,
    out,
    keys, values, qbuf, obuf, ostat, xr, xs, yb, ystat, yr, ys, ab, rb, gs, gb, wo, wh,
    pb, cb, zs, zr, ez, ea, ex, ya, xa, lg, fz, fy, fx, fg,
    local_sem, send_sem, recv_sem,
):
    X, Y, Z = sizes
    S, R, W = q.shape
    heads = W // HEAD_SIZE
    ZH = Z // 2
    cols = pb.shape[-1]
    ctx, tp = lax.axis_index("ctx"), lax.axis_index("tp")
    x, y = ctx // Y, lax.rem(ctx, Y)
    z, k = tp // 2, lax.rem(tp, 2)
    zh, s_own = z // 2, lax.rem(z, 2)
    z_other = z + 1 - 2 * s_own

    def on_x(d):
        return (lax.rem(x + d + X, X) * Y + y, tp)

    def on_y(d):
        return (x * Y + lax.rem(y + d + Y, Y), tp)

    def on_z(d):
        return (ctx, lax.rem(z + d + Z, Z) * 2 + k)

    def on_pair(j):
        return (ctx, (z_other if j >= 2 else z) * 2 + (1 - k if j % 2 else k))

    started = []

    def copy_of(i, src, dst, device):
        return pltpu.make_async_remote_copy(
            src_ref=src,
            dst_ref=dst,
            send_sem=send_sem.at[i],
            recv_sem=recv_sem.at[i],
            device_id=device,
            device_id_type=pl.DeviceIdType.MESH,
        )

    def send(src, dst, device):
        copy = copy_of(len(started), src, dst, device)
        copy.start()
        started.append(copy)
        return len(started) - 1

    def recv(i, dst):
        copy_of(i, dst, dst, on_pair(1)).wait_recv()

    x_order, y_order, z_order = near_first(X), near_first(Y), near_first(Z)
    zh_order = near_first(ZH)

    barrier = pltpu.get_barrier_semaphore()
    peers = [on_y(d) for d in y_order] + [on_x(d) for d in x_order] + [on_z(d) for d in z_order]
    peers += [on_pair(1), on_pair(3)]
    for peer in peers:
        pl.semaphore_signal(
            barrier, inc=1, device_id=peer, device_id_type=pl.DeviceIdType.MESH
        )
    local = [
        pltpu.make_async_copy(keys_hbm, keys, local_sem.at[0]),
        pltpu.make_async_copy(values_hbm, values, local_sem.at[1]),
        pltpu.make_async_copy(proj_hbm, wo.at[y], local_sem.at[2]),
        pltpu.make_async_copy(head_hbm, wh.at[:, 0:128], local_sem.at[3]),
    ]
    for copy in local:
        copy.start()

    for s in range(S):
        for h in range(heads):
            at = slice(h * HEAD_SIZE, (h + 1) * HEAD_SIZE)
            part = q[s, :, at].astype(F32)
            turned = part * cosine[s] + pltpu.roll(part, HEAD_SIZE // 2, 1) * sine[s]
            qbuf[0, 0, s, :, at] = turned.astype(BF16)
    gs[k] = gain[...]
    rb[x] = resid[...]
    pl.semaphore_wait(barrier, len(peers))

    sent_y = {d: send(qbuf.at[0, 0], qbuf.at[0, d], on_y(d)) for d in y_order}
    sent_x = {}
    for e in x_order:
        sent_x[e, 0] = send(qbuf.at[0, 0], qbuf.at[e, 0], on_x(e))
    sent_gain = send(gs.at[k], gs.at[k], on_pair(1))
    local[3].wait()
    sent_head = {j: send(wh.at[:, 0:128], wh.at[:, j * 128 : (j + 1) * 128], on_pair(j)) for j in (2, 1)}
    for d in y_order:
        recv(sent_y[d], qbuf.at[0, d])
        for e in x_order:
            sent_x[e, d] = send(qbuf.at[0, d], qbuf.at[e, d], on_x(e))
    local[2].wait()
    sent_proj = {d: send(wo.at[y], wo.at[y], on_y(d)) for d in y_order}
    sent_resid = {e: send(rb.at[x], rb.at[x], on_x(e)) for e in x_order}

    scale = 1.0 / math.sqrt(HEAD_SIZE)
    group = Y * R

    def attend(e):
        logs = []
        for s in range(S):
            for h in range(heads):
                at = slice(h * HEAD_SIZE, (h + 1) * HEAD_SIZE)
                block = qbuf[e, :, s, :, at].reshape(group, HEAD_SIZE)
                scores = lax.dot_general(
                    block, keys[s, :, at], (((1,), (1,)), ((), ())), preferred_element_type=F32
                ) * scale
                top = jnp.max(scores, -1, keepdims=True)
                weights = jnp.exp(scores - top)
                total = jnp.sum(weights, -1, keepdims=True)
                summed = jnp.dot(
                    weights.astype(BF16), values[s, :, at], preferred_element_type=F32
                )
                obuf[e, s, :, at] = (summed / total).astype(BF16)
                logs.append(top + jnp.log(total))
        ostat[e] = columns_to_tile(logs)

    local[0].wait()
    local[1].wait()
    attend(0)
    recv(sent_gain, gs.at[1 - k])
    gb[z] = gs[...]
    sent_gains = {d: send(gs, gb.at[z], on_z(d)) for d in z_order}
    sent_o, sent_s = {}, {}
    for e in x_order:
        for d in [0] + y_order:
            recv(sent_x[e, d], qbuf.at[e, d])
        attend(e)
        sent_o[e] = send(obuf.at[e], xr.at[e], on_x(-e))
        sent_s[e] = send(ostat.at[e], xs.at[e], on_x(-e))
    for e in x_order:
        recv(sent_o[e], xr.at[e])
        recv(sent_s[e], xs.at[e])

    shares, log_sum = merge([ostat[0]] + [xs[e] for e in x_order])
    table = transposed(shares)
    for s in range(S):
        for h in range(heads):
            at = slice(h * HEAD_SIZE, (h + 1) * HEAD_SIZE)
            total = None
            for place, e in enumerate([0] + x_order):
                column = place * 8 + s * heads + h
                part = obuf[0, s, :, at] if e == 0 else xr[e, s, :, at]
                part = part.astype(F32) * table[:group, column : column + 1]
                total = part if total is None else total + part
            yb[:, s, :, at] = total.reshape(Y, R, HEAD_SIZE).astype(BF16)
    ystat[...] = log_sum
    sent_o, sent_s = {}, {}
    for d in y_order:
        sent_o[d] = send(yb.at[d], yr.at[d], on_y(-d))
        sent_s[d] = send(ystat, ys.at[d], on_y(-d))
    recv(sent_head[2], wh.at[:, 256:384])
    sent_head[3] = send(wh.at[:, 256:384], wh.at[:, 384:512], on_pair(1))
    for d in y_order:
        recv(sent_o[d], yr.at[d])
        recv(sent_s[d], ys.at[d])
    shares, _ = merge([ystat[...]] + [pltpu.roll(ys[d], 128 - d * R, 1) for d in y_order])
    table = transposed(shares)
    for s in range(S):
        for h in range(heads):
            at = slice(h * HEAD_SIZE, (h + 1) * HEAD_SIZE)
            total = None
            for place, d in enumerate([0] + y_order):
                column = place * 8 + s * heads + h
                part = yb[0, s, :, at] if d == 0 else yr[d, s, :, at]
                part = part.astype(F32) * table[:R, column : column + 1]
                total = part if total is None else total + part
            ab[x, s, :, at] = total.astype(BF16)

    sent = {e: send(ab.at[x], ab.at[x], on_x(e)) for e in x_order}
    for d in y_order:
        recv(sent_proj[d], wo.at[lax.rem(y - d + Y, Y)])
    for e in x_order:
        recv(sent_resid[e], rb.at[lax.rem(x - e + X, X)])
    for e in x_order:
        recv(sent[e], ab.at[lax.rem(x - e + X, X)])
    rows = X * S * R
    attended = ab[...].reshape(rows, W)
    residual = rb[...].reshape(rows, W).astype(F32)
    width = wo.shape[-1]
    for j in range(cols // W):
        if width < W:
            each = W // width
            weights = jnp.concatenate([wo[j * each + i] for i in range(each)], axis=1)
        else:
            first = j * W
            weights = wo[first // width, :, first % width : first % width + W]
        mine = (tp == x * (cols // W) + j).astype(F32)
        part = jnp.dot(attended, weights, preferred_element_type=F32) + residual * mine
        part = part.reshape(X * S, 2, R // 2, W)
        for half in range(2):
            pb[half, :, :, j * W : (j + 1) * W] = part[:, half]

    sent_core = send(pb.at[1 - k], cb, on_pair(1))
    recv(sent_core, cb)
    zs[...] = pb[k] + cb[...]
    sent = {d: send(zs.at[lax.rem(z + d, Z)], zr.at[d], on_z(d)) for d in z_order}
    for d in z_order:
        recv(sent_gains[d], gb.at[lax.rem(z - d + Z, Z)])
    stream = zs[z]
    for d in z_order:
        recv(sent[d], zr.at[d])
        stream = stream + zr[d]
    squares = jnp.sum(stream * stream, -1, keepdims=True)
    gains = [gb[x * (cols // W // 2) + j // 2, j % 2] for j in range(cols // W)]
    scaled = stream * jnp.concatenate(gains, axis=1)
    half = cols // 2
    ez[zh] = jnp.concatenate([scaled[:, :half], scaled[:, half:]], axis=0).astype(BF16)
    lane = lax.broadcasted_iota(jnp.int32, (R // 2, 128), 1)
    own_target = target[s_own, pl.ds(pl.multiple_of(k * (R // 2), R // 2), R // 2), :]
    own_target = own_target * (x == zh).astype(F32)
    ea[zh] = jnp.where(lane == 0, squares, jnp.where(lane == 1, own_target, 0.0))

    sent, sent_a = {}, {}
    for e in zh_order:
        sent[e] = send(ez.at[zh], ez.at[zh], on_z(2 * e))
        sent_a[e] = send(ea.at[zh], ea.at[zh], on_z(2 * e))
    for e in zh_order:
        recv(sent[e], ez.at[lax.rem(zh - e + ZH, ZH)])
        recv(sent_a[e], ea.at[lax.rem(zh - e + ZH, ZH)])
    unstacked = []
    for i in range(ZH):
        both = ez[i].astype(F32)
        unstacked.append(jnp.concatenate([both[: R // 2], both[R // 2 :]], axis=1))
    ex[x, y] = jnp.concatenate(unstacked, axis=0).astype(BF16)
    ya[y] = transposed([ea[i] for i in range(ZH)])[:8]
    sent = {d: send(ex.at[x, y], ex.at[x, y], on_y(d)) for d in y_order}
    sent_a = {d: send(ya.at[y], ya.at[y], on_y(d)) for d in y_order}
    sent_x = {}
    for e in x_order:
        sent_x[e, 0] = send(ex.at[x, y], ex.at[x, y], on_x(e))
    for d in y_order:
        from_y = lax.rem(y - d + Y, Y)
        recv(sent[d], ex.at[x, from_y])
        for e in x_order:
            sent_x[e, d] = send(ex.at[x, from_y], ex.at[x, from_y], on_x(e))
    for d in y_order:
        recv(sent_a[d], ya.at[lax.rem(y - d + Y, Y)])
    block = ZH * (R // 2)
    per_tile = 128 // block
    tiles = xa.shape[1]
    for i in range(tiles):
        total = None
        for place in range(min(per_tile, Y)):
            tile = ya[i * per_tile + place]
            if place:
                tile = pltpu.roll(tile, place * block, 1)
            total = tile if total is None else total + tile
        xa[x, i] = total
    sent_a = {e: send(xa.at[x], xa.at[x], on_x(e)) for e in x_order}

    recv(sent_head[1], wh.at[:, 128:256])
    recv(sent_head[3], wh.at[:, 384:512])
    slots = Y * block
    for e in [0] + x_order:
        from_x = lax.rem(x - e + X, X)
        if e:
            for d in [0] + y_order:
                recv(sent_x[e, d], ex.at[from_x, lax.rem(y - d + Y, Y)])
        part = jnp.dot(
            ex[from_x].reshape(slots, cols),
            wh[pl.ds(pl.multiple_of(from_x * cols, cols), cols), :],
            preferred_element_type=F32,
        )
        if e:
            lg[...] += part
        else:
            lg[...] = part
    for e in x_order:
        recv(sent_a[e], xa.at[lax.rem(x - e + X, X)])
    span = min(128, slots)
    for i in range(tiles):
        total = xa[0, i]
        for from_x in range(1, X):
            total = total + xa[from_x, i]
        table = transposed([lax.rsqrt(total * (1.0 / (X * cols)) + NORM_EPSILON), total])
        logits = lg[i * span : (i + 1) * span, :] * table[:span, 0:1]
        wanted = table[:span, 9:10]
        top = jnp.max(logits, -1, keepdims=True)
        sums = jnp.sum(jnp.exp(logits - top), -1, keepdims=True)
        lane = lax.broadcasted_iota(jnp.int32, (span, 128), 1)
        picked = jnp.zeros((span, 128), F32)
        for j in range(4):
            first = (ctx * (2 * Z) + on_pair(j)[1]) * 128
            hit = (lane + first).astype(F32) == wanted
            picked = picked + jnp.where(hit, logits[:, j * 128 : (j + 1) * 128], 0.0)
        fz[zh, i] = columns_to_tile(
            [top + jnp.log(sums), jnp.sum(picked, -1, keepdims=True)]
        )

    def combine(ref, count):
        parts = [ref[i] for i in range(count)]
        _, log_sum = merge(parts)
        row = lax.broadcasted_iota(jnp.int32, parts[0].shape, 1)
        return jnp.where(row == 0, log_sum, functools.reduce(jnp.add, parts))

    sent = {e: send(fz.at[zh], fz.at[zh], on_z(2 * e)) for e in zh_order}
    for e in zh_order:
        recv(sent[e], fz.at[lax.rem(zh - e + ZH, ZH)])
    fy[y] = combine(fz, ZH)
    sent = {d: send(fy.at[y], fy.at[y], on_y(d)) for d in y_order}
    for d in y_order:
        recv(sent[d], fy.at[lax.rem(y - d + Y, Y)])
    fx[x] = combine(fy, Y)
    sent = {e: send(fx.at[x], fx.at[x], on_x(e)) for e in x_order}
    for e in x_order:
        recv(sent[e], fx.at[lax.rem(x - e + X, X)])
    here = s_own * 2 + k
    fg[here] = combine(fx, X)
    sent = {j: send(fg.at[here], fg.at[here], on_pair(j)) for j in (1, 2, 3)}
    for j in (1, 2, 3):
        recv(sent[j], fg.at[(1 - s_own if j >= 2 else s_own) * 2 + (1 - k if j % 2 else k)])
    out[...] = fg[:, :, 0:1, :] - fg[:, :, 1:2, :]
    for copy in started:
        copy.wait_send()


def copies(X, Y, Z):
    x, y, z, zh = X - 1, Y - 1, Z - 1, Z // 2 - 1
    count = y + x + 1 + 2 + x * y + y + x + z + 2 * x + 2 * y + 1 + x + 1 + z
    return count + 2 * zh + 2 * y + x + x * y + x + zh + y + x + 3


def on_device(
    sizes,
    queries,
    positions,
    cached_keys,
    cached_values,
    residual_rows,
    out_proj,
    norm_gain,
    head_weight,
    targets,
    live_rows,
    mask_total,
):
    X, Y, Z = sizes
    S, R, W = queries.shape
    L = cached_keys.shape[1]
    D = head_weight.shape[0]
    cols = D // X
    ZH = Z // 2
    block = ZH * (R // 2)
    tiles = -(-Y * block // 128)
    frequency = ROPE_BASE ** (-2.0 * jnp.arange(HEAD_SIZE // 2, dtype=F32) / HEAD_SIZE)
    frequency = jnp.concatenate([frequency, frequency])
    sign = jnp.concatenate([-jnp.ones(HEAD_SIZE // 2, F32), jnp.ones(HEAD_SIZE // 2, F32)])
    angles = positions.astype(F32)[..., None] * frequency
    cosine, sine = jnp.cos(angles), jnp.sin(angles) * sign
    target = jnp.broadcast_to(targets.astype(F32)[..., None], (S, R, 128))
    gain = jnp.broadcast_to(norm_gain.astype(F32)[None], (8, W))
    vmem = pl.BlockSpec(memory_space=pltpu.VMEM)
    hbm = pl.BlockSpec(memory_space=pl.ANY)
    scratch = [
        ((S, L, W), BF16),
        ((S, L, W), BF16),
        ((X, Y, S, R, W), BF16),
        ((X, S, Y * R, W), BF16),
        ((X, 8, 128), F32),
        ((X, S, Y * R, W), BF16),
        ((X, 8, 128), F32),
        ((Y, S, R, W), BF16),
        ((8, 128), F32),
        ((Y, S, R, W), BF16),
        ((Y, 8, 128), F32),
        ((X, S, R, W), BF16),
        ((X, S, R, W), BF16),
        ((2, 8, W), F32),
        ((Z, 2, 8, W), F32),
        ((Y, W, out_proj.shape[1]), BF16),
        ((D, 4 * 128), BF16),
        ((2, Z, R // 2, cols), F32),
        ((Z, R // 2, cols), F32),
        ((Z, R // 2, cols), F32),
        ((Z, R // 2, cols), F32),
        ((ZH, R, cols // 2), BF16),
        ((ZH, R // 2, 128), F32),
        ((X, Y, block, cols), BF16),
        ((Y, 8, 128), F32),
        ((X, tiles, 8, 128), F32),
        ((Y * block, 4 * 128), F32),
        ((ZH, tiles, 8, 128), F32),
        ((Y, tiles, 8, 128), F32),
        ((X, tiles, 8, 128), F32),
        ((4, tiles, 8, 128), F32),
    ]
    count = copies(X, Y, Z)
    nll = pl.pallas_call(
        functools.partial(kernel, sizes),
        out_shape=jax.ShapeDtypeStruct((4, tiles, 1, 128), F32),
        in_specs=[vmem] * 6 + [hbm] * 4,
        out_specs=vmem,
        scratch_shapes=[pltpu.VMEM(*shape) for shape in scratch]
        + [
            pltpu.SemaphoreType.DMA((4,)),
            pltpu.SemaphoreType.DMA((count,)),
            pltpu.SemaphoreType.DMA((count,)),
        ],
        compiler_params=pltpu.CompilerParams(
            collective_id=0, has_side_effects=True, vmem_limit_bytes=44 * 1024 * 1024
        ),
        name="cloze",
    )(queries, cosine, sine, target, residual_rows, gain, cached_keys, cached_values, out_proj, head_weight)
    nll = nll.reshape(S, 2, -1, X, R // 2)[:, :, :Y]
    nll = jnp.transpose(nll, (0, 3, 2, 1, 4)).reshape(S, X * Y * R)
    alive = jnp.arange(X * Y * R, dtype=jnp.int32)[None, :] < live_rows[:, None]
    nll = jnp.where(alive, nll, 0.0)
    elbo_estimate = jnp.sum(jnp.sum(nll, 1) / mask_total.astype(F32)) / S
    token_nll = lax.dynamic_slice_in_dim(nll, lax.axis_index("ctx") * R, R, 1)
    return (token_nll, elbo_estimate)


def solution(mesh):
    Z = mesh.shape["tp"] // 2
    X = Z // 2
    sizes = (X, mesh.shape["ctx"] // X, Z)
    in_specs = (
        P(None, "ctx", "tp"),
        P(None, "ctx"),
        P(None, "ctx", "tp"),
        P(None, "ctx", "tp"),
        P(None, "ctx", "tp"),
        P("tp", "ctx"),
        P("tp"),
        P(None, ("ctx", "tp")),
        P(None, "ctx"),
        P(),
        P(),
    )
    return jax.shard_map(
        functools.partial(on_device, sizes),
        mesh=mesh,
        in_specs=in_specs,
        out_specs=(P(None, "ctx"), P()),
        check_vma=False,
    )
```

```python
import functools
import heapq
import math

import jax
import jax.numpy as jnp
from jax import lax
from jax.experimental import pallas as pl
from jax.experimental.pallas import tpu as pltpu
from jax.sharding import PartitionSpec as P

HEAD_SIZE = 128
ROPE_BASE = 500000.0
NORM_EPSILON = 1e-05
F32 = jnp.float32
BF16 = jnp.bfloat16


def near_first(n):
    return sorted(range(1, n), key=lambda d: (min(d, n - d), d))


def transposed(tiles):
    stacked = jnp.concatenate(tiles, axis=0)
    if stacked.shape[0] < 128:
        stacked = jnp.concatenate(
            [stacked, jnp.zeros((128 - stacked.shape[0], 128), F32)], axis=0
        )
    return stacked.T


def columns_to_tile(columns):
    rows = next(iter(columns.values())).shape[0]
    lane = lax.broadcasted_iota(jnp.int32, (rows, 128), 1)
    table = jnp.zeros((rows, 128), F32)
    for at, column in columns.items():
        table = jnp.where(lane == at, column, table)
    if rows < 128:
        table = jnp.concatenate([table, jnp.zeros((128 - rows, 128), F32)], axis=0)
    return table.T[:8]


def merge(tiles):
    top = functools.reduce(jnp.maximum, tiles)
    weights = [jnp.exp(tile - top) for tile in tiles]
    total = functools.reduce(jnp.add, weights)
    return [weight / total for weight in weights], top + jnp.log(total)


def kernel(
    sizes,
    live_rows, mask_total,
    q_hbm, positions_hbm, frequency_hbm, targets_hbm, resid_hbm, gain_hbm,
    keys_hbm, values_hbm, proj_hbm, head_hbm,
    out, loss,
    q, positions, frequency, targets, gain, keys, values, qbuf, obuf, ostat, xr, xs, yb, ystat, yr, ys, ab, rb, gs, gb, wo, wh,
    pb, cb, tt, zs, zr, ea, ex, ya, xa, lg, ft, fy, fx,
    local_sem, send_sem, recv_sem,
):
    X, Y, Z = sizes
    S, R, W = q_hbm.shape
    heads = W // HEAD_SIZE
    ZH = Z // 2
    cols = pb.shape[-1]
    ctx, tp = lax.axis_index("ctx"), lax.axis_index("tp")
    x, y = ctx // Y, lax.rem(ctx, Y)
    z, k = tp // 2, lax.rem(tp, 2)
    zh, s_own = z // 2, lax.rem(z, 2)
    z_other = z + 1 - 2 * s_own

    def on_x(d):
        return (lax.rem(x + d + X, X) * Y + y, tp)

    def on_y(d):
        return (x * Y + lax.rem(y + d + Y, Y), tp)

    def on_z(d):
        return (ctx, lax.rem(z + d + Z, Z) * 2 + k)

    def on_pair(j):
        return (ctx, (z_other if j >= 2 else z) * 2 + (1 - k if j % 2 else k))

    started = []

    def copy_of(i, src, dst, device):
        return pltpu.make_async_remote_copy(
            src_ref=src,
            dst_ref=dst,
            send_sem=send_sem.at[i],
            recv_sem=recv_sem.at[i],
            device_id=device,
            device_id_type=pl.DeviceIdType.MESH,
        )

    def send(src, dst, device):
        copy = copy_of(len(started), src, dst, device)
        copy.start()
        started.append(copy)
        return len(started) - 1

    def recv(i, dst):
        copy_of(i, dst, dst, on_pair(1)).wait_recv()

    def on_tp(d):
        return (ctx, lax.rem(tp + d, 2 * Z))

    x_order, y_order, z_order = near_first(X), near_first(Y), near_first(Z)
    zh_order = near_first(ZH)

    fetched = [
        (q_hbm, q), (positions_hbm, positions), (frequency_hbm, frequency),
        (head_hbm, wh.at[:, 0:128]), (targets_hbm, targets), (gain_hbm, gain),
        (resid_hbm, rb.at[x]), (keys_hbm, keys), (values_hbm, values), (proj_hbm, wo.at[y]),
    ]
    local = [
        pltpu.make_async_copy(src, dst, local_sem.at[i]) for i, (src, dst) in enumerate(fetched)
    ]
    for copy in local:
        copy.start()

    barrier = pltpu.get_barrier_semaphore()
    peers = [on_y(d) for d in y_order] + [on_x(d) for d in x_order]
    peers += [on_tp(d) for d in range(1, 2 * Z)]
    for peer in peers:
        pl.semaphore_signal(
            barrier, inc=1, device_id=peer, device_id_type=pl.DeviceIdType.MESH
        )

    def column_table(ref):
        table = jnp.concatenate([ref[...].astype(F32), jnp.zeros((S, 128 - R), F32)], axis=1)
        return transposed([jnp.concatenate([table, jnp.zeros((8 - S, 128), F32)], axis=0)])

    for copy in local[:3]:
        copy.wait()
    places = column_table(positions)
    lane = lax.broadcasted_iota(jnp.int32, (R, HEAD_SIZE), 1)
    for s in range(S):
        angles = places[:R, s : s + 1] * frequency[...]
        cosine, sine = jnp.cos(angles), jnp.sin(angles)
        sine = jnp.where(lane < HEAD_SIZE // 2, -sine, sine)
        for h in range(heads):
            at = slice(h * HEAD_SIZE, (h + 1) * HEAD_SIZE)
            part = q[s, :, at].astype(F32)
            turned = part * cosine + pltpu.roll(part, HEAD_SIZE // 2, 1) * sine
            qbuf[0, 0, s, :, at] = turned.astype(BF16)
    for copy in local[3:6]:
        copy.wait()
    gs[k] = jnp.broadcast_to(gain[...].astype(F32).reshape(1, W), (8, W))
    wanted = column_table(targets)
    for s in range(S):
        tt[s] = jnp.broadcast_to(wanted[:R, s : s + 1], (R, 128))
    pl.semaphore_wait(barrier, len(peers))

    sent_y = {d: send(qbuf.at[0, 0], qbuf.at[0, d], on_y(d)) for d in y_order}
    sent_x = {}
    sides = {1: [], 2: [1]}.get(X, [1, X - 1])
    for e in sides:
        sent_x[e, 0] = send(qbuf.at[0, 0], qbuf.at[e, 0], on_x(e))
    sent_gain = send(gs.at[k], gs.at[k], on_pair(1))
    sent_head = {j: send(wh.at[:, 0:128], wh.at[:, j * 128 : (j + 1) * 128], on_pair(j)) for j in (2, 1)}
    for d in y_order:
        recv(sent_y[d], qbuf.at[0, d])
        for e in sides:
            sent_x[e, d] = send(qbuf.at[0, d], qbuf.at[e, d], on_x(e))
    for e in x_order[len(sides) :]:
        for d in [0] + y_order:
            sent_x[e, d] = send(qbuf.at[0, d], qbuf.at[e, d], on_x(e))
    for copy in local[6:]:
        copy.wait()
    sent_proj = {d: send(wo.at[y], wo.at[y], on_y(d)) for d in y_order}
    sent_resid = {e: send(rb.at[x], rb.at[x], on_x(e)) for e in x_order}

    scale = math.log2(math.e) / math.sqrt(HEAD_SIZE)
    group = Y * R

    def attend(e, s):
        logs = {}
        for h in range(heads):
            at = slice(h * HEAD_SIZE, (h + 1) * HEAD_SIZE)
            block = qbuf[e, :, s, :, at].reshape(group, HEAD_SIZE)
            scores = lax.dot_general(
                block, keys[s, :, at], (((1,), (1,)), ((), ())), preferred_element_type=F32
            )
            top = jnp.max(scores, -1, keepdims=True)
            weights = jnp.exp2((scores - top) * scale)
            total = jnp.sum(weights, -1, keepdims=True)
            summed = jnp.dot(
                weights.astype(BF16), values[s, :, at], preferred_element_type=F32
            )
            obuf[e, s, :, at] = (summed / total).astype(BF16)
            logs[s * heads + h] = top * (1.0 / math.sqrt(HEAD_SIZE)) + jnp.log(total)
        ostat[e, s] = columns_to_tile(logs)

    for s in range(S):
        attend(0, s)
    recv(sent_gain, gs.at[1 - k])
    gb[z] = gs[...]
    sent_gains = {d: send(gs, gb.at[z], on_z(d)) for d in z_order}
    sent_o, sent_s = {}, {}
    units = [(e, s) for s in range(S) for e in sides]
    for e, s in units + [(e, s) for e in x_order[len(sides) :] for s in range(S)]:
        if s == 0:
            for d in [0] + y_order:
                recv(sent_x[e, d], qbuf.at[e, d])
        attend(e, s)
        sent_o[e, s] = send(obuf.at[e, s], xr.at[e, s], on_x(-e))
        sent_s[e, s] = send(ostat.at[e, s], xs.at[e, s], on_x(-e))

    sent_yo, sent_ys, log_sums = {}, {}, []
    for s in range(S):
        for e in x_order:
            recv(sent_o[e, s], xr.at[e, s])
            recv(sent_s[e, s], xs.at[e, s])
        shares, log_sum = merge([ostat[0, s]] + [xs[e, s] for e in x_order])
        log_sums.append(log_sum)
        table = transposed(shares)
        for h in range(heads):
            at = slice(h * HEAD_SIZE, (h + 1) * HEAD_SIZE)
            total = None
            for place, e in enumerate([0] + x_order):
                column = place * 8 + s * heads + h
                part = obuf[0, s, :, at] if e == 0 else xr[e, s, :, at]
                part = part.astype(F32) * table[:group, column : column + 1]
                total = part if total is None else total + part
            yb[s, :, :, at] = total.reshape(Y, R, HEAD_SIZE).astype(BF16)
        for d in y_order:
            sent_yo[d, s] = send(yb.at[s, d], yr.at[s, d], on_y(-d))
    row = lax.broadcasted_iota(jnp.int32, (8, 128), 0)
    ystat[...] = jnp.where(row < heads, log_sums[0], log_sums[1])
    for d in y_order:
        sent_ys[d] = send(ystat, ys.at[d], on_y(-d))
    for d in y_order:
        recv(sent_ys[d], ys.at[d])
    shares, _ = merge([ystat[...]] + [pltpu.roll(ys[d], 128 - d * R, 1) for d in y_order])
    table = transposed(shares)
    for s in range(S):
        for d in y_order:
            recv(sent_yo[d, s], yr.at[s, d])
        for h in range(heads):
            at = slice(h * HEAD_SIZE, (h + 1) * HEAD_SIZE)
            total = None
            for place, d in enumerate([0] + y_order):
                column = place * 8 + s * heads + h
                part = yb[s, 0, :, at] if d == 0 else yr[s, d, :, at]
                part = part.astype(F32) * table[:R, column : column + 1]
                total = part if total is None else total + part
            ab[x, s, :, at] = total.astype(BF16)

    sent = {e: send(ab.at[x], ab.at[x], on_x(e)) for e in x_order}
    for d in y_order:
        recv(sent_proj[d], wo.at[lax.rem(y - d + Y, Y)])
    for e in x_order:
        recv(sent_resid[e], rb.at[lax.rem(x - e + X, X)])
    for e in x_order:
        recv(sent[e], ab.at[lax.rem(x - e + X, X)])
    rows = X * S * R
    attended = ab[...].reshape(rows, W)
    residual = rb[...].reshape(rows, W).astype(F32)
    width = wo.shape[-1]
    for j in range(cols // W):
        if width < W:
            each = W // width
            weights = jnp.concatenate([wo[j * each + i] for i in range(each)], axis=1)
        else:
            first = j * W
            weights = wo[first // width, :, first % width : first % width + W]
        mine = (tp == x * (cols // W) + j).astype(F32)
        part = jnp.dot(attended, weights, preferred_element_type=F32) + residual * mine
        part = part.reshape(X * S, 2, R // 2, W)
        for half in range(2):
            pb[half, :, :, j * W : (j + 1) * W] = part[:, half]

    eight, half = R // 2, cols // 2
    sent_core = send(pb.at[1 - k], cb, on_pair(1))
    recv(sent_core, cb)
    summed = pb[k] + cb[...]
    zs[...] = jnp.concatenate([summed[:, :, :half], summed[:, :, half:]], axis=1).astype(BF16)
    sent = {d: send(zs.at[lax.rem(z + d, Z)], zr.at[d], on_z(d)) for d in z_order}
    for d in z_order:
        recv(sent_gains[d], gb.at[lax.rem(z - d + Z, Z)])
    stream = pb[k, z] + cb[z]
    for d in z_order:
        recv(sent[d], zr.at[d])
        both = zr[d].astype(F32)
        stream = stream + jnp.concatenate([both[:eight], both[eight:]], axis=1)
    gains = [gb[x * (cols // W // 2) + j // 2, j % 2] for j in range(cols // W)]
    scaled = stream * jnp.concatenate(gains, axis=1)
    ex[x, y, zh] = jnp.concatenate([scaled[:, :half], scaled[:, half:]], axis=0).astype(BF16)

    def near(e):
        return lax.rem(zh - e + ZH, ZH)

    def piece(i, d, e):
        return ex.at[lax.rem(x - i + X, X), lax.rem(y - d + Y, Y), near(e)]

    y_direct = [d for d in y_order if Y < 8 or min(d, Y - d) <= 2]
    z_steps = [0] + zh_order
    under_way, busy = [], {}

    def launch(now, axis, step, i, d, e):
        size = {"x": X, "y": Y, "z": ZH}[axis]
        device = {"x": on_x, "y": on_y, "z": lambda n: on_z(2 * n)}[axis](step)
        number = send(piece(i, d, e), piece(i, d, e), device)
        way = step % size
        way = way if 2 * way <= size else way - size
        link = (axis, way > 0)
        busy[link] = max(now, busy.get(link, 0.0)) + 0.35 * abs(way)
        there = [i, d, e]
        at = "xyz".index(axis)
        there[at] = (there[at] + step) % size
        hops = abs(way) * (2 if axis == "z" else 1)
        heapq.heappush(under_way, (busy[link] + 1.4 + 0.7 * hops, number, tuple(there)))

    def spread_y(now, i, d, e):
        if d == 0:
            for step in y_direct:
                launch(now, "y", step, i, d, e)
        elif Y == 8 and d in (2, Y - 2):
            step = 1 if d == 2 else -1
            launch(now, "y", step, i, d, e)
            if (i + e + (step > 0)) % 2:
                launch(now, "y", 2 * step, i, d, e)

    def arrived(now, i, d, e):
        if e == 0 or i == 0:
            spread_y(now, i, d, e)
        if e and i == 0:
            for step in sides:
                launch(now, "x", step, i, d, e)
        elif e and X == 4 and i == (1 if (z_steps.index(e) + d) % 2 else X - 1):
            launch(now, "x", 1 if i == 1 else -1, i, d, e)

    for e in zh_order:
        launch(0.0, "z", e, 0, 0, 0)
    for i in x_order:
        launch(0.0, "x", i, 0, 0, 0)
    spread_y(0.0, 0, 0, 0)
    lane = lax.broadcasted_iota(jnp.int32, (eight, 128), 1)
    squares = jnp.sum(stream * stream, -1, keepdims=True)
    wanted = tt[s_own, pl.ds(pl.multiple_of(k * eight, eight), eight), :] * (x == zh).astype(F32)
    ea[zh] = jnp.where(lane == 0, squares, jnp.where(lane == 1, wanted, 0.0))
    sent_az = {e: send(ea.at[zh], ea.at[zh], on_z(2 * e)) for e in zh_order}
    recv(sent_head[2], wh.at[:, 256:384])
    sent_head[3] = send(wh.at[:, 256:384], wh.at[:, 384:512], on_pair(1))

    block = ZH * eight
    per_tile = 128 // block
    tiles = xa.shape[1]
    sent_ay, sent_ax = {}, {}

    def rows_along_y():
        for e in zh_order:
            recv(sent_az[e], ea.at[near(e)])
        ya[y] = transposed([ea[i] for i in range(ZH)])[:8]
        for d in y_order:
            sent_ay[d] = send(ya.at[y], ya.at[y], on_y(d))

    def rows_along_x():
        for d in y_order:
            recv(sent_ay[d], ya.at[lax.rem(y - d + Y, Y)])
        for i in range(tiles):
            total = None
            for place in range(min(per_tile, Y)):
                tile = ya[i * per_tile + place]
                if place:
                    tile = pltpu.roll(tile, place * block, 1)
                total = tile if total is None else total + tile
            xa[x, i] = total
        for e in x_order:
            sent_ax[e] = send(xa.at[x], xa.at[x], on_x(e))

    slots = Y * ZH * eight

    def multiply(i):
        if not complete:
            for j in (1, 3):
                recv(sent_head[j], wh.at[:, j * 128 : (j + 1) * 128])
        from_x = lax.rem(x - i + X, X)
        block = ex[from_x].reshape(Y * ZH * R, half)
        total = None
        for upper in range(2):
            start = pl.multiple_of(from_x * cols + upper * half, half)
            part = jnp.dot(block, wh[pl.ds(start, half), :], preferred_element_type=F32)
            part = part.reshape(Y * ZH, 2, eight, 4 * 128)[:, upper]
            total = part if total is None else total + part
        total = total.reshape(slots, 4 * 128)
        if complete:
            lg[...] += total
        else:
            lg[...] = total
        complete.append(i)

    complete = []
    missing = {i: Y * ZH for i in range(X)}
    missing[0] -= 1
    later = [(6.0, rows_along_y), (11.0, rows_along_x)]
    while under_way:
        now, number, place = heapq.heappop(under_way)
        while later and later[0][0] < now:
            later.pop(0)[1]()
        recv(number, piece(*place))
        arrived(now, *place)
        missing[place[0]] -= 1
        if missing[place[0]] == 0 and under_way:
            multiply(place[0])
    for _, step in later:
        step()
    for i in range(X):
        if i not in complete:
            multiply(i)
    for e in x_order:
        recv(sent_ax[e], xa.at[lax.rem(x - e + X, X)])
    span = min(128, slots)
    fin = None
    for i in range(tiles):
        total = xa[0, i]
        for from_x in range(1, X):
            total = total + xa[from_x, i]
        table = transposed([lax.rsqrt(total * (1.0 / (X * cols)) + NORM_EPSILON), total])
        logits = lg[i * span : (i + 1) * span, :] * table[:span, 0:1]
        wanted = table[:span, 9:10]
        top = jnp.max(logits, -1, keepdims=True)
        sums = jnp.sum(jnp.exp(logits - top), -1, keepdims=True)
        lane = lax.broadcasted_iota(jnp.int32, (span, 128), 1)
        picked = jnp.zeros((span, 128), F32)
        for j in range(4):
            first = (ctx * (2 * Z) + on_pair(j)[1]) * 128
            hit = (lane + first).astype(F32) == wanted
            picked = picked + jnp.where(hit, logits[:, j * 128 : (j + 1) * 128], 0.0)
        tile = columns_to_tile(
            {i: top + jnp.log(sums), 4 + i: jnp.sum(picked, -1, keepdims=True)}
        )
        fin = tile if fin is None else fin + tile
    ft[tp] = fin

    def combine(parts):
        _, log_sum = merge(parts)
        row = lax.broadcasted_iota(jnp.int32, (8, 128), 0)
        return jnp.where(row < 4, log_sum, functools.reduce(jnp.add, parts))

    sent = {d: send(ft.at[tp], ft.at[tp], on_tp(d)) for d in range(1, 2 * Z)}
    for d in range(1, 2 * Z):
        recv(sent[d], ft.at[lax.rem(tp - d + 2 * Z, 2 * Z)])
    for s in range(S):
        first, second = (
            combine([ft[4 * i + 2 * s + core] for i in range(ZH)]) for core in range(2)
        )
        fy[y, s] = jnp.where(lax.rem(row, 4) < 2, first, pltpu.roll(second, 2, 0))
    sent = {d: send(fy.at[y], fy.at[y], on_y(d)) for d in y_order}
    for d in y_order:
        recv(sent[d], fy.at[lax.rem(y - d + Y, Y)])
    for s in range(S):
        fx[x, s] = combine([fy[i, s] for i in range(Y)])
    sent = {e: send(fx.at[x], fx.at[x], on_x(e)) for e in x_order}
    for e in x_order:
        recv(sent[e], fx.at[lax.rem(x - e + X, X)])

    lane = lax.broadcasted_iota(jnp.int32, (8, 128), 1)
    from_y = lax.rem(row, 2) * per_tile + lane // block
    from_x = lax.rem(lane, block) // eight
    slot = (from_x * Y + from_y) * R + (row // 2) * eight + lax.rem(lane, eight)
    counted = (row < 4) & (from_y < Y)
    sample_sum, own = None, []
    first = lax.rem(y, per_tile) * block + x * eight
    member = lax.broadcasted_iota(jnp.int32, (R, 128), 0)
    place = lax.broadcasted_iota(jnp.int32, (R, 128), 1) == first + lax.rem(member, eight)
    for s in range(S):
        tile = combine([fx[i, s] for i in range(X)])
        tile = tile - pltpu.roll(tile, 4, 0)
        tile = jnp.where(counted & (slot < live_rows[s]), tile, 0.0)
        total = jnp.sum(jnp.sum(tile, 1, keepdims=True), 0, keepdims=True)
        total = total / jnp.full((1, 1), mask_total[s], jnp.int32).astype(F32)
        sample_sum = total if sample_sum is None else sample_sum + total
        in_first = y < per_tile
        lower = jnp.where(in_first, tile[0:1], tile[1:2])
        upper = jnp.where(in_first, tile[2:3], tile[3:4])
        own.append(jnp.where(place, jnp.where(member < eight, lower, upper), 0.0))
    loss[...] = sample_sum * (1.0 / S)
    token = jnp.sum(transposed(own), 0, keepdims=True)
    for s in range(S):
        out[s : s + 1, :] = token[:, s * R : (s + 1) * R]
    for copy in started:
        copy.wait_send()
    assert len(started) == copies(X, Y, Z), len(started)


def copies(X, Y, Z):
    x, y, z, zh = X - 1, Y - 1, Z - 1, Z // 2 - 1
    count = y + x + 1 + 2 + x * y + y + x + z + 4 * x + 3 * y + x + 1 + z
    count += X * Y * Z // 2 - 1 + 1 + zh + y + x
    return count + 2 * Z - 1 + y + x


def on_device(
    sizes,
    queries,
    positions,
    cached_keys,
    cached_values,
    residual_rows,
    out_proj,
    norm_gain,
    head_weight,
    targets,
    live_rows,
    mask_total,
):
    X, Y, Z = sizes
    S, R, W = queries.shape
    L = cached_keys.shape[1]
    D = head_weight.shape[0]
    cols = D // X
    ZH = Z // 2
    block = ZH * (R // 2)
    tiles = -(-Y * block // 128)
    frequency = ROPE_BASE ** (-2.0 * jnp.arange(HEAD_SIZE // 2, dtype=F32) / HEAD_SIZE)
    frequency = jnp.concatenate([frequency, frequency])[None]
    vmem = pl.BlockSpec(memory_space=pltpu.VMEM)
    hbm = pl.BlockSpec(memory_space=pl.ANY)
    scratch = [
        ((S, R, W), BF16),
        ((S, R), jnp.int32),
        ((1, HEAD_SIZE), F32),
        ((S, R), jnp.int32),
        ((W,), BF16),
        ((S, L, W), BF16),
        ((S, L, W), BF16),
        ((X, Y, S, R, W), BF16),
        ((X, S, Y * R, W), BF16),
        ((X, S, 8, 128), F32),
        ((X, S, Y * R, W), BF16),
        ((X, S, 8, 128), F32),
        ((S, Y, R, W), BF16),
        ((8, 128), F32),
        ((S, Y, R, W), BF16),
        ((Y, 8, 128), F32),
        ((X, S, R, W), BF16),
        ((X, S, R, W), BF16),
        ((2, 8, W), F32),
        ((Z, 2, 8, W), F32),
        ((Y, W, out_proj.shape[1]), BF16),
        ((D, 4 * 128), BF16),
        ((2, Z, R // 2, cols), F32),
        ((Z, R // 2, cols), F32),
        ((S, R, 128), F32),
        ((Z, R, cols // 2), BF16),
        ((Z, R, cols // 2), BF16),
        ((ZH, R // 2, 128), F32),
        ((X, Y, ZH, R, cols // 2), BF16),
        ((Y, 8, 128), F32),
        ((X, tiles, 8, 128), F32),
        ((Y * block, 4 * 128), F32),
        ((2 * Z, 8, 128), F32),
        ((Y, S, 8, 128), F32),
        ((X, S, 8, 128), F32),
    ]
    count = copies(X, Y, Z)
    smem = pl.BlockSpec(memory_space=pltpu.SMEM)
    token_nll, loss = pl.pallas_call(
        functools.partial(kernel, sizes),
        out_shape=[jax.ShapeDtypeStruct((S, R), F32), jax.ShapeDtypeStruct((1, 1), F32)],
        in_specs=[smem] * 2 + [hbm] * 10,
        out_specs=[vmem, vmem],
        scratch_shapes=[pltpu.VMEM(*shape) for shape in scratch]
        + [
            pltpu.SemaphoreType.DMA((10,)),
            pltpu.SemaphoreType.DMA((count,)),
            pltpu.SemaphoreType.DMA((count,)),
        ],
        compiler_params=pltpu.CompilerParams(
            collective_id=0, has_side_effects=True, vmem_limit_bytes=60 * 1024 * 1024
        ),
        name="cloze",
    )(
        live_rows, mask_total, queries, positions, frequency, targets, residual_rows,
        norm_gain, cached_keys, cached_values, out_proj, head_weight,
    )
    return (token_nll, loss.reshape(()))


def solution(mesh):
    Z = mesh.shape["tp"] // 2
    X = Z // 2
    sizes = (X, mesh.shape["ctx"] // X, Z)
    in_specs = (
        P(None, "ctx", "tp"),
        P(None, "ctx"),
        P(None, "ctx", "tp"),
        P(None, "ctx", "tp"),
        P(None, "ctx", "tp"),
        P("tp", "ctx"),
        P("tp"),
        P(None, ("ctx", "tp")),
        P(None, "ctx"),
        P(),
        P(),
    )
    return jax.shard_map(
        functools.partial(on_device, sizes),
        mesh=mesh,
        in_specs=in_specs,
        out_specs=(P(None, "ctx"), P()),
        check_vma=False,
    )
```

```python
import functools
import heapq
import math

import jax
import jax.numpy as jnp
from jax import lax
from jax.experimental import pallas as pl
from jax.experimental.pallas import tpu as pltpu
from jax.sharding import PartitionSpec as P

HEAD_SIZE = 128
ROPE_BASE = 500000.0
NORM_EPSILON = 1e-05
F32 = jnp.float32
BF16 = jnp.bfloat16


def near_first(n):
    return sorted(range(1, n), key=lambda d: (min(d, n - d), d))


def transposed(tiles):
    stacked = jnp.concatenate(tiles, axis=0)
    if stacked.shape[0] < 128:
        stacked = jnp.concatenate(
            [stacked, jnp.zeros((128 - stacked.shape[0], 128), F32)], axis=0
        )
    return stacked.T


def columns_to_tile(columns):
    rows = next(iter(columns.values())).shape[0]
    lane = lax.broadcasted_iota(jnp.int32, (rows, 128), 1)
    table = jnp.zeros((rows, 128), F32)
    for at, column in columns.items():
        table = jnp.where(lane == at, column, table)
    if rows < 128:
        table = jnp.concatenate([table, jnp.zeros((128 - rows, 128), F32)], axis=0)
    return table.T[:8]


def merge(tiles):
    top = functools.reduce(jnp.maximum, tiles)
    weights = [jnp.exp(tile - top) for tile in tiles]
    total = functools.reduce(jnp.add, weights)
    return [weight / total for weight in weights], top + jnp.log(total)


def kernel(
    sizes,
    live_hbm, mask_hbm, q_hbm, positions_hbm, targets_hbm, resid_hbm, gain_hbm,
    keys_hbm, values_hbm, proj_hbm, head_hbm,
    out, loss,
    live_rows, mask_total, q, positions, targets, resid, gain, keys, values, qbuf, obuf, ostat,
    xr, xs, yb, ystat, yr, ys, ab, at_x, rb, gs, gb, wo, wh, own, tt, zs, zr, ea, ex, ya, xa, lg, ft, fy, fx,
    local_sem, send_sem, recv_sem,
):
    X, Y, Z = sizes
    S, R, W = q_hbm.shape
    heads = W // HEAD_SIZE
    ZH = Z // 2
    cols = own.shape[-1]
    ctx, tp = lax.axis_index("ctx"), lax.axis_index("tp")
    x, y = ctx // Y, lax.rem(ctx, Y)
    z, k = tp // 2, lax.rem(tp, 2)
    zh, parity = z // 2, lax.rem(z, 2)
    z_other = z + 1 - 2 * parity

    def on_x(d):
        return (lax.rem(x + d + X, X) * Y + y, tp)

    def on_y(d):
        return (x * Y + lax.rem(y + d + Y, Y), tp)

    def on_z(d):
        return (ctx, lax.rem(z + d + Z, Z) * 2 + k)

    def on_pair(j):
        return (ctx, (z_other if j >= 2 else z) * 2 + (1 - k if j % 2 else k))

    started = []

    def copy_of(i, src, dst, device):
        return pltpu.make_async_remote_copy(
            src_ref=src,
            dst_ref=dst,
            send_sem=send_sem.at[i],
            recv_sem=recv_sem.at[i],
            device_id=device,
            device_id_type=pl.DeviceIdType.MESH,
        )

    def send(src, dst, device):
        copy = copy_of(len(started), src, dst, device)
        copy.start()
        started.append(copy)
        return len(started) - 1

    def recv(i, dst):
        copy_of(i, dst, dst, on_pair(1)).wait_recv()

    def on_tp(d):
        return (ctx, lax.rem(tp + d, 2 * Z))

    def other_core(device):
        return (device[0], z * 2 + 1 - k)

    x_order, y_order, z_order = near_first(X), near_first(Y), near_first(Z)
    zh_order = near_first(ZH)

    fetched = [
        (positions_hbm, positions), (q_hbm, q),
        (head_hbm, wh.at[:, 0:128]), (targets_hbm, targets), (gain_hbm, gain),
        (live_hbm, live_rows), (mask_hbm, mask_total),
        (resid_hbm, resid), (keys_hbm, keys), (values_hbm, values), (proj_hbm, wo.at[k, y]),
    ]
    local = [
        pltpu.make_async_copy(src, dst, local_sem.at[i]) for i, (src, dst) in enumerate(fetched)
    ]
    for copy in local:
        copy.start()

    barrier = pltpu.get_barrier_semaphore()
    peers = [on_y(d) for d in y_order] + [on_x(d) for d in x_order]
    peers += [on_tp(d) for d in range(1, 2 * Z)]
    peers += [other_core(on_x(d)) for d in x_order]
    for peer in peers:
        pl.semaphore_signal(
            barrier, inc=1, device_id=peer, device_id_type=pl.DeviceIdType.MESH
        )

    def column_table(ref):
        table = jnp.concatenate([ref[...].astype(F32), jnp.zeros((S, 128 - R), F32)], axis=1)
        return transposed([jnp.concatenate([table, jnp.zeros((8 - S, 128), F32)], axis=0)])

    lane = lax.broadcasted_iota(jnp.int32, (R, HEAD_SIZE), 1)
    place = lax.rem(lane, HEAD_SIZE // 2).astype(F32)
    frequency = ROPE_BASE ** (-2.0 * place / HEAD_SIZE)
    local[0].wait()
    places = column_table(positions)
    angles = [places[:R, s : s + 1] * frequency for s in range(S)]
    turns = [(jnp.cos(angle), jnp.sin(angle)) for angle in angles]
    local[1].wait()
    for s in range(S):
        cosine, sine = turns[s]
        sine = jnp.where(lane < HEAD_SIZE // 2, -sine, sine)
        for h in range(heads):
            at = slice(h * HEAD_SIZE, (h + 1) * HEAD_SIZE)
            part = q[s, :, at].astype(F32)
            turned = part * cosine + pltpu.roll(part, HEAD_SIZE // 2, 1) * sine
            qbuf[s, 0, 0, :, at] = turned.astype(BF16)
    for copy in local[2:5]:
        copy.wait()
    gs[k] = jnp.broadcast_to(gain[...].astype(F32).reshape(1, W), (8, W))
    wanted = column_table(targets)
    for s in range(S):
        tt[s] = jnp.broadcast_to(wanted[:R, s : s + 1], (R, 128))
    pl.semaphore_wait(barrier, len(peers))

    scale = math.log2(math.e) / math.sqrt(HEAD_SIZE)
    group = Y * R

    def attend(members, s):
        logs = [{} for _ in members]
        for h in range(heads):
            at = slice(h * HEAD_SIZE, (h + 1) * HEAD_SIZE)
            block = [qbuf[s, e, :, :, at].reshape(group, HEAD_SIZE) for e in members]
            scores = lax.dot_general(
                jnp.concatenate(block, axis=0),
                keys[s, :, at],
                (((1,), (1,)), ((), ())),
                preferred_element_type=F32,
            )
            top = jnp.max(scores, -1, keepdims=True)
            weights = jnp.exp2((scores - top) * scale)
            total = jnp.sum(weights, -1, keepdims=True)
            summed = jnp.dot(
                weights.astype(BF16), values[s, :, at], preferred_element_type=F32
            )
            summed = (summed / total).astype(BF16)
            log_sum = top * (1.0 / math.sqrt(HEAD_SIZE)) + jnp.log(total)
            for place, e in enumerate(members):
                rows = slice(place * group, (place + 1) * group)
                obuf[e, s, :, at] = summed[rows]
                logs[place][h] = log_sum[rows]
        for place, e in enumerate(members):
            ostat[e, s] = columns_to_tile(logs[place])[:heads]

    def attend_first():
        attend([0], 0)

    sides = {1: [], 2: [1]}.get(X, [1, X - 1])
    opposite, y_steps = x_order[len(sides) :], [0] + y_order
    sent_y, sent_x = {}, {}
    for s in range(S):
        for d in y_order:
            sent_y[s, d] = send(qbuf.at[s, 0, 0], qbuf.at[s, 0, d], on_y(d))
    sent_gain = send(gs.at[k], gs.at[k], on_pair(1))
    sent_head = {j: send(wh.at[:, 0:128], wh.at[:, j * 128 : (j + 1) * 128], on_pair(j)) for j in (2, 1)}

    def queries_on(s, ways, d):
        for e in ways:
            sent_x[s, e, d] = send(qbuf.at[s, 0, d], qbuf.at[s, e, d], on_x(e))

    for s in range(S):
        queries_on(s, sides, 0)
        for at, d in enumerate(y_order):
            recv(sent_y[s, d], qbuf.at[s, 0, d])
            queries_on(s, sides, d)
            if at >= 2:
                queries_on(s, opposite, y_steps[at - 2])
        for d in y_steps[max(Y - 3, 0) :]:
            queries_on(s, opposite, d)
        if s == 0:
            for copy in local[5:]:
                copy.wait()
            attend_first()
    y_direct = [d for d in y_order if Y < 8 or min(d, Y - d) <= 2]
    sent_proj = {d: send(wo.at[k, y], wo.at[k, y], on_y(d)) for d in reversed(y_direct)}

    def proj_from(d):
        return wo.at[k, lax.rem(y - d + Y, Y)]

    def half_of(ref, first):
        return ref.at[: W // 2] if first else ref.at[W // 2 :]


    def spread_x(numbers, block, slots, s):
        @pl.when(k == s)
        def _():
            slots[x, k] = block[s]
            for e in x_order:
                copy_of(numbers["same", e], block.at[s], slots.at[x, k], on_x(e)).start()

        @pl.when(k != s)
        def _():
            for e in [0] + x_order:
                there = other_core(on_x(e))
                copy_of(numbers["other", e], block.at[s], slots.at[x, k], there).start()

    def numbers_for(block, slots):
        numbers = {}
        for way, steps in (("same", x_order), ("other", [0] + x_order)):
            for e in steps:
                numbers[way, e] = len(started)
                started.append(copy_of(len(started), block.at[0], slots.at[x, k], on_pair(1)))
        return numbers

    def gathered_x(numbers, slots):
        for (way, e), number in numbers.items():
            recv(number, slots.at[lax.rem(x - e + X, X), k if way == "same" else 1 - k])

    sent_resid = numbers_for(resid, rb)
    for s in range(S):
        spread_x(sent_resid, resid, rb, s)

    sent_o, sent_s = {}, {}

    def attend_others(members, s):
        for e in members:
            for d in y_steps:
                recv(sent_x[s, e, d], qbuf.at[s, e, d])
        if members:
            attend(members, s)
        for e in members:
            sent_o[e, s] = send(obuf.at[e, s], xr.at[e, s], on_x(-e))
            sent_s[e, s] = send(ostat.at[e, s], xs.at[e, s], on_x(-e))

    attend_others(sides, 0)
    attend_others(opposite, 0)
    recv(sent_gain, gs.at[1 - k])
    gb[z] = gs[...]
    sent_gains = {d: send(gs, gb.at[z], on_z(d)) for d in z_order}
    attend_others(sides, 1)
    attend([0], 1)
    attend_others(opposite, 1)

    for d in y_direct:
        recv(sent_proj[d], proj_from(d))
    if Y == 8:
        for step, d in ((1, 2), (-1, Y - 2)):
            sent_proj[d + step] = send(proj_from(d), proj_from(d), on_y(step))
        for step, d in ((2, 2), (-2, Y - 2)):
            part = (step > 0, Y // 2)
            sent_proj[part] = send(*[half_of(proj_from(d), step > 0)] * 2, on_y(step))

    sent_yo, sent_ys = {}, {}
    for s in range(S):
        for e in x_order:
            recv(sent_o[e, s], xr.at[e, s])
            recv(sent_s[e, s], xs.at[e, s])
        shares, ystat[s] = merge([ostat[0, s]] + [xs[e, s] for e in x_order])
        table = transposed(shares)
        for h in range(heads):
            at = slice(h * HEAD_SIZE, (h + 1) * HEAD_SIZE)
            total = None
            for place, e in enumerate([0] + x_order):
                column = place * heads + h
                part = obuf[0, s, :, at] if e == 0 else xr[e, s, :, at]
                part = part.astype(F32) * table[:group, column : column + 1]
                total = part if total is None else total + part
            yb[s, :, :, at] = total.reshape(Y, R, HEAD_SIZE).astype(BF16)
        for d in y_order:
            sent_yo[d, s] = send(yb.at[s, d], yr.at[s, d], on_y(-d))
            sent_ys[d, s] = send(ystat.at[s], ys.at[s, d], on_y(-d))
    if Y == 8:
        for d in (3, Y - 3):
            recv(sent_proj[d], proj_from(d))
        for first in (True, False):
            recv(sent_proj[first, Y // 2], half_of(proj_from(Y // 2), first))
    sent_proj = send(wo.at[k], wo.at[k], on_pair(1))
    sent_rows = numbers_for(ab, at_x)
    for s in range(S):
        for d in y_order:
            recv(sent_yo[d, s], yr.at[s, d])
            recv(sent_ys[d, s], ys.at[s, d])
        shares, _ = merge([ystat[s]] + [pltpu.roll(ys[s, d], 128 - d * R, 1) for d in y_order])
        table = transposed(shares)
        for h in range(heads):
            at = slice(h * HEAD_SIZE, (h + 1) * HEAD_SIZE)
            total = None
            for place, d in enumerate([0] + y_order):
                column = place * heads + h
                part = yb[s, 0, :, at] if d == 0 else yr[s, d, :, at]
                part = part.astype(F32) * table[:R, column : column + 1]
                total = part if total is None else total + part
            ab[s, :, at] = total.astype(BF16)
        spread_x(sent_rows, ab, at_x, s)

    recv(sent_proj, wo.at[1 - k])
    gathered_x(sent_resid, rb)
    gathered_x(sent_rows, at_x)
    eight, half = R // 2, cols // 2
    attended = jnp.concatenate([at_x[:, c].reshape(X * R, W) for c in range(2)], axis=1)
    width = wo.shape[-1]
    for j in range(cols // W):
        weights = []
        for c in range(2):
            if width < W:
                each = W // width
                weights.append(
                    jnp.concatenate([wo[c, j * each + i] for i in range(each)], axis=1)
                )
            else:
                first = j * W
                weights.append(wo[c, first // width, :, first % width : first % width + W])
        part = jnp.dot(attended, jnp.concatenate(weights, axis=0), preferred_element_type=F32)
        block = x * (cols // W) + j
        mine = (z == block // 2).astype(F32)
        part = part + rb[:, j % 2].reshape(X * R, W).astype(F32) * mine
        own[:, :, j * W : (j + 1) * W] = part.reshape(Z, eight, W)

    summed = own[...]
    zs[...] = jnp.concatenate([summed[:, :, :half], summed[:, :, half:]], axis=1).astype(BF16)
    sent = {d: send(zs.at[lax.rem(z + d, Z)], zr.at[d], on_z(d)) for d in z_order}
    for d in z_order:
        recv(sent_gains[d], gb.at[lax.rem(z - d + Z, Z)])
    stream = own[z]
    for d in z_order:
        recv(sent[d], zr.at[d])
        both = zr[d].astype(F32)
        stream = stream + jnp.concatenate([both[:eight], both[eight:]], axis=1)
    gains = [gb[x * (cols // W // 2) + j // 2, j % 2] for j in range(cols // W)]
    scaled = stream * jnp.concatenate(gains, axis=1)
    ex[x, y, zh] = jnp.concatenate([scaled[:, :half], scaled[:, half:]], axis=0).astype(BF16)

    def near(e):
        return lax.rem(zh - e + ZH, ZH)

    def piece(i, d, e):
        return ex.at[lax.rem(x - i + X, X), lax.rem(y - d + Y, Y), near(e)]

    z_steps = [0] + zh_order
    x_first = z_steps[-1]
    under_way, busy = [], {}

    def launch(now, axis, step, i, d, e):
        size = {"x": X, "y": Y, "z": ZH}[axis]
        device = {"x": on_x, "y": on_y, "z": lambda n: on_z(2 * n)}[axis](step)
        number = send(piece(i, d, e), piece(i, d, e), device)
        way = step % size
        way = way if 2 * way <= size else way - size
        link = (axis, way > 0)
        busy[link] = max(now, busy.get(link, 0.0)) + 0.35 * abs(way)
        there = [i, d, e]
        at = "xyz".index(axis)
        there[at] = (there[at] + step) % size
        hops = abs(way) * (2 if axis == "z" else 1)
        heapq.heappush(under_way, (busy[link] + 1.4 + 0.7 * hops, number, tuple(there)))

    def spread_y(now, i, d, e):
        if d == 0:
            for step in y_direct:
                launch(now, "y", step, i, d, e)
        elif Y == 8 and d in (2, Y - 2):
            step = 1 if d == 2 else -1
            launch(now, "y", step, i, d, e)
            if (i + e + (step > 0)) % 2:
                launch(now, "y", 2 * step, i, d, e)

    def arrived(now, i, d, e):
        if e == x_first and i == d == 0:
            for step in x_order:
                launch(now, "x", step, i, d, e)
        elif e != x_first and i == 0:
            for step in sides:
                launch(now, "x", step, i, d, e)
        if e == x_first or i == 0:
            spread_y(now, i, d, e)
        elif X == 4 and i == (1 if (z_steps.index(e) + d) % 2 else X - 1):
            launch(now, "x", 1 if i == 1 else -1, i, d, e)

    for e in zh_order:
        launch(0.0, "z", e, 0, 0, 0)
    arrived(0.0, 0, 0, 0)
    lane = lax.broadcasted_iota(jnp.int32, (eight, 128), 1)
    squares = jnp.sum(stream * stream, -1, keepdims=True)
    wanted = tt[k, pl.ds(pl.multiple_of(parity * eight, eight), eight), :] * (x == zh).astype(F32)
    ea[zh] = jnp.where(lane == 0, squares, jnp.where(lane == 1, wanted, 0.0))
    sent_az = {e: send(ea.at[zh], ea.at[zh], on_z(2 * e)) for e in zh_order}
    recv(sent_head[2], wh.at[:, 256:384])
    sent_head[3] = send(wh.at[:, 256:384], wh.at[:, 384:512], on_pair(1))

    block = ZH * eight
    per_tile = 128 // block
    tiles = xa.shape[1]
    sent_ay, sent_ax = {}, {}

    def rows_along_y():
        for e in zh_order:
            recv(sent_az[e], ea.at[near(e)])
        ya[y] = transposed([ea[i] for i in range(ZH)])[:8]
        for d in y_order:
            sent_ay[d] = send(ya.at[y], ya.at[y], on_y(d))

    def rows_along_x():
        for d in y_order:
            recv(sent_ay[d], ya.at[lax.rem(y - d + Y, Y)])
        for i in range(tiles):
            total = None
            for place in range(min(per_tile, Y)):
                tile = ya[i * per_tile + place]
                if place:
                    tile = pltpu.roll(tile, place * block, 1)
                total = tile if total is None else total + tile
            xa[x, i] = total
        for e in x_order:
            sent_ax[e] = send(xa.at[x], xa.at[x], on_x(e))

    slots = Y * ZH * eight

    def multiply(i):
        if not complete:
            for j in (1, 3):
                recv(sent_head[j], wh.at[:, j * 128 : (j + 1) * 128])
        from_x = lax.rem(x - i + X, X)
        block = ex[from_x].reshape(Y * ZH * R, half)
        total = None
        for upper in range(2):
            start = pl.multiple_of(from_x * cols + upper * half, half)
            part = jnp.dot(block, wh[pl.ds(start, half), :], preferred_element_type=F32)
            part = part.reshape(Y * ZH, 2, eight, 4 * 128)[:, upper]
            total = part if total is None else total + part
        total = total.reshape(slots, 4 * 128)
        if complete:
            lg[...] += total
        else:
            lg[...] = total
        complete.append(i)

    complete = []
    missing = {i: Y * ZH for i in range(X)}
    missing[0] -= 1
    later = [(6.0, rows_along_y), (11.0, rows_along_x)]
    while under_way:
        now, number, place = heapq.heappop(under_way)
        while later and later[0][0] < now:
            later.pop(0)[1]()
        recv(number, piece(*place))
        arrived(now, *place)
        missing[place[0]] -= 1
        if missing[place[0]] == 0 and under_way:
            multiply(place[0])
    for _, step in later:
        step()
    for i in range(X):
        if i not in complete:
            multiply(i)
    for e in x_order:
        recv(sent_ax[e], xa.at[lax.rem(x - e + X, X)])
    span = min(128, slots)
    fin = None
    for i in range(tiles):
        total = xa[0, i]
        for from_x in range(1, X):
            total = total + xa[from_x, i]
        table = transposed([lax.rsqrt(total * (1.0 / (X * cols)) + NORM_EPSILON), total])
        logits = lg[i * span : (i + 1) * span, :] * table[:span, 0:1]
        wanted = table[:span, 9:10]
        top = jnp.max(logits, -1, keepdims=True)
        sums = jnp.sum(jnp.exp(logits - top), -1, keepdims=True)
        lane = lax.broadcasted_iota(jnp.int32, (span, 128), 1)
        picked = jnp.zeros((span, 128), F32)
        for j in range(4):
            first = (ctx * (2 * Z) + on_pair(j)[1]) * 128
            hit = (lane + first).astype(F32) == wanted
            picked = picked + jnp.where(hit, logits[:, j * 128 : (j + 1) * 128], 0.0)
        tile = columns_to_tile(
            {i: top + jnp.log(sums), 2 + i: jnp.sum(picked, -1, keepdims=True)}
        )
        fin = tile if fin is None else fin + tile
    ft[tp] = fin[:4]

    row = lax.broadcasted_iota(jnp.int32, (8, 128), 0)

    def combine(parts):
        _, log_sum = merge(parts)
        logs = lax.broadcasted_iota(jnp.int32, parts[0].shape, 0) < parts[0].shape[0] // 2
        return jnp.where(logs, log_sum, functools.reduce(jnp.add, parts))

    sent = {d: send(ft.at[tp], ft.at[tp], on_tp(d)) for d in range(1, 2 * Z)}
    settled = len(started)
    for copy in started:
        copy.wait_send()
    for d in range(1, 2 * Z):
        recv(sent[d], ft.at[lax.rem(tp - d + 2 * Z, 2 * Z)])
    for s in range(S):
        first, second = (
            combine([ft[4 * i + 2 * upper + s] for i in range(ZH)]) for upper in range(2)
        )
        fy[y, s] = jnp.concatenate([first[:2], second[:2], first[2:], second[2:]], axis=0)
    sent = {d: send(fy.at[y], fy.at[y], on_y(d)) for d in y_order}
    for d in y_order:
        recv(sent[d], fy.at[lax.rem(y - d + Y, Y)])
    for s in range(S):
        fx[x, s] = combine([fy[i, s] for i in range(Y)])
    sent = {e: send(fx.at[x], fx.at[x], on_x(e)) for e in x_order}
    for e in x_order:
        recv(sent[e], fx.at[lax.rem(x - e + X, X)])

    lane = lax.broadcasted_iota(jnp.int32, (8, 128), 1)
    from_y = lax.rem(row, 2) * per_tile + lane // block
    from_x = lax.rem(lane, block) // eight
    slot = (from_x * Y + from_y) * R + (row // 2) * eight + lax.rem(lane, eight)
    counted = (row < 4) & (from_y < Y)
    sample_sum, tokens = None, []
    first = lax.rem(y, per_tile) * block + x * eight
    member = lax.broadcasted_iota(jnp.int32, (R, 128), 0)
    place = lax.broadcasted_iota(jnp.int32, (R, 128), 1) == first + lax.rem(member, eight)
    for s in range(S):
        tile = combine([fx[i, s] for i in range(X)])
        tile = tile - pltpu.roll(tile, 4, 0)
        tile = jnp.where(counted & (slot < live_rows[s]), tile, 0.0)
        total = jnp.sum(jnp.sum(tile, 1, keepdims=True), 0, keepdims=True)
        total = total / jnp.full((1, 1), mask_total[s], jnp.int32).astype(F32)
        sample_sum = total if sample_sum is None else sample_sum + total
        in_first = y < per_tile
        lower = jnp.where(in_first, tile[0:1], tile[1:2])
        upper = jnp.where(in_first, tile[2:3], tile[3:4])
        tokens.append(jnp.where(place, jnp.where(member < eight, lower, upper), 0.0))
    loss[...] = sample_sum * (1.0 / S)
    token = jnp.sum(transposed(tokens), 0, keepdims=True)
    for s in range(S):
        out[0, s : s + 1, :] = token[:, s * R : (s + 1) * R]
    for copy in started[settled:]:
        copy.wait_send()
    assert len(started) == copies(X, Y, Z), len(started)


def copies(X, Y, Z):
    x, y, z, zh = X - 1, Y - 1, Z - 1, Z // 2 - 1
    count = 2 * (y + x + x * y) + 3 + (8 if Y == 8 else y) + 2 * (2 * x + 1) + z + 4 * x + 4 * y + 1 + z
    count += X * Y * Z // 2 - 1 + 1 + zh + y + x
    return count + 2 * Z - 1 + y + x


def on_device(
    sizes,
    queries,
    positions,
    cached_keys,
    cached_values,
    residual_rows,
    out_proj,
    norm_gain,
    head_weight,
    targets,
    live_rows,
    mask_total,
):
    X, Y, Z = sizes
    S, R, W = queries.shape
    L = cached_keys.shape[1]
    D = head_weight.shape[0]
    cols = D // X
    ZH = Z // 2
    block = ZH * (R // 2)
    tiles = -(-Y * block // 128)
    vmem = pl.BlockSpec(memory_space=pltpu.VMEM)
    hbm = pl.BlockSpec(memory_space=pl.ANY)
    scratch = [
        ((S, R, W), BF16),
        ((S, R), jnp.int32),
        ((S, R), jnp.int32),
        ((S, R, W), BF16),
        ((W,), BF16),
        ((S, L, W), BF16),
        ((S, L, W), BF16),
        ((S, X, Y, R, W), BF16),
        ((X, S, Y * R, W), BF16),
        ((X, S, W // HEAD_SIZE, 128), F32),
        ((X, S, Y * R, W), BF16),
        ((X, S, W // HEAD_SIZE, 128), F32),
        ((S, Y, R, W), BF16),
        ((S, W // HEAD_SIZE, 128), F32),
        ((S, Y, R, W), BF16),
        ((S, Y, W // HEAD_SIZE, 128), F32),
        ((S, R, W), BF16),
        ((X, 2, R, W), BF16),
        ((X, 2, R, W), BF16),
        ((2, 8, W), F32),
        ((Z, 2, 8, W), F32),
        ((2, Y, W, out_proj.shape[1]), BF16),
        ((D, 4 * 128), BF16),
        ((Z, R // 2, cols), F32),
        ((S, R, 128), F32),
        ((Z, R, cols // 2), BF16),
        ((Z, R, cols // 2), BF16),
        ((ZH, R // 2, 128), F32),
        ((X, Y, ZH, R, cols // 2), BF16),
        ((Y, 8, 128), F32),
        ((X, tiles, 8, 128), F32),
        ((Y * block, 4 * 128), F32),
        ((2 * Z, 4, 128), F32),
        ((Y, S, 8, 128), F32),
        ((X, S, 8, 128), F32),
    ]
    count = copies(X, Y, Z)
    token_nll, loss = pl.pallas_call(
        functools.partial(kernel, sizes),
        out_shape=[jax.ShapeDtypeStruct((1, S, R), F32), jax.ShapeDtypeStruct((1, 1), F32)],
        in_specs=[hbm] * 11,
        out_specs=[vmem, vmem],
        scratch_shapes=[pltpu.SMEM((S,), jnp.int32)] * 2
        + [pltpu.VMEM(*shape) for shape in scratch]
        + [
            pltpu.SemaphoreType.DMA((11,)),
            pltpu.SemaphoreType.DMA((count,)),
            pltpu.SemaphoreType.DMA((count,)),
        ],
        compiler_params=pltpu.CompilerParams(
            collective_id=0, has_side_effects=True, vmem_limit_bytes=60 * 1024 * 1024
        ),
        name="cloze",
    )(
        live_rows, mask_total, queries, positions, targets, residual_rows,
        norm_gain, cached_keys, cached_values, out_proj, head_weight,
    )
    return (token_nll.reshape(S, R), loss.reshape(()))


def solution(mesh):
    Z = mesh.shape["tp"] // 2
    X = Z // 2
    sizes = (X, mesh.shape["ctx"] // X, Z)
    in_specs = (
        P(None, "ctx", "tp"),
        P(None, "ctx"),
        P(None, "ctx", "tp"),
        P(None, "ctx", "tp"),
        P(None, "ctx", "tp"),
        P("tp", "ctx"),
        P("tp"),
        P(None, ("ctx", "tp")),
        P(None, "ctx"),
        P(),
        P(),
    )
    return jax.shard_map(
        functools.partial(on_device, sizes),
        mesh=mesh,
        in_specs=in_specs,
        out_specs=(P(None, "ctx"), P()),
        check_vma=False,
    )
```

```python
import functools
import heapq
import math

import jax
import jax.numpy as jnp
from jax import lax
from jax.experimental import pallas as pl
from jax.experimental.pallas import tpu as pltpu
from jax.sharding import PartitionSpec as P

HEAD_SIZE = 128
ROPE_BASE = 500000.0
NORM_EPSILON = 1e-05
F32 = jnp.float32
BF16 = jnp.bfloat16


def near_first(n):
    return sorted(range(1, n), key=lambda d: (min(d, n - d), d))


def transposed(tiles):
    stacked = jnp.concatenate(tiles, axis=0)
    if stacked.shape[0] < 128:
        stacked = jnp.concatenate(
            [stacked, jnp.zeros((128 - stacked.shape[0], 128), F32)], axis=0
        )
    return stacked.T


def columns_to_tile(columns):
    rows = next(iter(columns.values())).shape[0]
    lane = lax.broadcasted_iota(jnp.int32, (rows, 128), 1)
    table = jnp.zeros((rows, 128), F32)
    for at, column in columns.items():
        table = jnp.where(lane == at, column, table)
    if rows < 128:
        table = jnp.concatenate([table, jnp.zeros((128 - rows, 128), F32)], axis=0)
    return table.T[:8]


def merge(tiles):
    top = functools.reduce(jnp.maximum, tiles)
    weights = [jnp.exp(tile - top) for tile in tiles]
    total = functools.reduce(jnp.add, weights)
    return [weight / total for weight in weights], top + jnp.log(total)


def kernel(
    sizes,
    live_hbm, mask_hbm, q_hbm, positions_hbm, targets_hbm, resid_hbm, gain_hbm,
    keys_hbm, values_hbm, proj_hbm, head_hbm,
    out_hbm, loss_hbm,
    live_rows, mask_total, q, positions, targets, resid, gain, keys, values, qbuf, obuf, ostat,
    xr, xs, yb, ystat, yr, ys, ab, at_x, rb, gb, wo, wh, own, tt, zs, zr, ea, ex, ya, xa, lg, ft, fy, fx, out, loss,
    local_sem, send_sem, recv_sem,
):
    X, Y, Z = sizes
    S, R, W = q_hbm.shape
    heads = W // HEAD_SIZE
    ZH = Z // 2
    cols = own.shape[-1]
    ctx, tp = lax.axis_index("ctx"), lax.axis_index("tp")
    x, y = ctx // Y, lax.rem(ctx, Y)
    z, k = tp // 2, lax.rem(tp, 2)
    zh, parity = z // 2, lax.rem(z, 2)
    z_other = z + 1 - 2 * parity

    def on_x(d):
        return (lax.rem(x + d + X, X) * Y + y, tp)

    def on_y(d):
        return (x * Y + lax.rem(y + d + Y, Y), tp)

    def on_z(d):
        return (ctx, lax.rem(z + d + Z, Z) * 2 + k)

    def on_pair(j):
        return (ctx, (z_other if j >= 2 else z) * 2 + (1 - k if j % 2 else k))

    started = []

    def copy_of(i, src, dst, device):
        return pltpu.make_async_remote_copy(
            src_ref=src,
            dst_ref=dst,
            send_sem=send_sem.at[i],
            recv_sem=recv_sem.at[i],
            device_id=device,
            device_id_type=pl.DeviceIdType.MESH,
        )

    def send(src, dst, device):
        copy = copy_of(len(started), src, dst, device)
        copy.start()
        started.append(copy)
        return len(started) - 1

    def recv(i, dst):
        copy_of(i, dst, dst, on_pair(1)).wait_recv()

    def on_tp(d):
        return (ctx, lax.rem(tp + d, 2 * Z))

    def other_core(device):
        return (device[0], z * 2 + 1 - k)

    x_order, y_order, z_order = near_first(X), near_first(Y), near_first(Z)
    zh_order = near_first(ZH)

    fetched = [
        (positions_hbm, positions), (q_hbm, q),
        (head_hbm, wh.at[:, 0:128]), (targets_hbm, targets), (gain_hbm, gain),
        (live_hbm, live_rows), (mask_hbm, mask_total),
        (resid_hbm, resid), (keys_hbm, keys), (values_hbm, values), (proj_hbm, wo.at[k, y]),
    ]
    local = [
        pltpu.make_async_copy(src, dst, local_sem.at[i]) for i, (src, dst) in enumerate(fetched)
    ]
    for copy in local:
        copy.start()

    barrier = pltpu.get_barrier_semaphore()
    peers = [on_y(d) for d in y_order] + [on_x(d) for d in x_order]
    peers += [on_tp(d) for d in range(1, 2 * Z)]
    peers += [other_core(on_x(d)) for d in x_order]
    for peer in peers:
        pl.semaphore_signal(
            barrier, inc=1, device_id=peer, device_id_type=pl.DeviceIdType.MESH
        )

    def column_table(ref):
        table = jnp.concatenate([ref[...].astype(F32), jnp.zeros((S, 128 - R), F32)], axis=1)
        return transposed([jnp.concatenate([table, jnp.zeros((8 - S, 128), F32)], axis=0)])

    lane = lax.broadcasted_iota(jnp.int32, (R, HEAD_SIZE), 1)
    place = lax.rem(lane, HEAD_SIZE // 2).astype(F32)
    frequency = ROPE_BASE ** (-2.0 * place / HEAD_SIZE)
    local[0].wait()
    places = column_table(positions)
    angles = [places[:R, s : s + 1] * frequency for s in range(S)]
    turns = [(jnp.cos(angle), jnp.sin(angle)) for angle in angles]
    local[1].wait()
    for s in range(S):
        cosine, sine = turns[s]
        sine = jnp.where(lane < HEAD_SIZE // 2, -sine, sine)
        for h in range(heads):
            at = slice(h * HEAD_SIZE, (h + 1) * HEAD_SIZE)
            part = q[s, :, at].astype(F32)
            turned = part * cosine + pltpu.roll(part, HEAD_SIZE // 2, 1) * sine
            qbuf[s, 0, 0, :, at] = turned.astype(BF16)
    for copy in local[2:5]:
        copy.wait()
    gb[tp] = gain[...].astype(F32).reshape(1, W)
    wanted = column_table(targets)
    for s in range(S):
        tt[s] = jnp.broadcast_to(wanted[:R, s : s + 1], (R, 128))
    pl.semaphore_wait(barrier, len(peers))

    scale = math.log2(math.e) / math.sqrt(HEAD_SIZE)
    group = Y * R

    def attend(members, s):
        logs = [{} for _ in members]
        for h in range(heads):
            at = slice(h * HEAD_SIZE, (h + 1) * HEAD_SIZE)
            block = [qbuf[s, e, :, :, at].reshape(group, HEAD_SIZE) for e in members]
            scores = lax.dot_general(
                jnp.concatenate(block, axis=0),
                keys[s, :, at],
                (((1,), (1,)), ((), ())),
                preferred_element_type=F32,
            )
            top = jnp.max(scores, -1, keepdims=True)
            weights = jnp.exp2((scores - top) * scale)
            total = jnp.sum(weights, -1, keepdims=True)
            summed = jnp.dot(
                weights.astype(BF16), values[s, :, at], preferred_element_type=F32
            )
            summed = (summed / total).astype(BF16)
            log_sum = top * (1.0 / math.sqrt(HEAD_SIZE)) + jnp.log(total)
            for place, e in enumerate(members):
                rows = slice(place * group, (place + 1) * group)
                obuf[e, s, :, at] = summed[rows]
                logs[place][h] = log_sum[rows]
        for place, e in enumerate(members):
            ostat[e, s] = columns_to_tile(logs[place])[:heads]

    def attend_first():
        attend([0], 0)

    sides = {1: [], 2: [1]}.get(X, [1, X - 1])
    opposite, y_steps = x_order[len(sides) :], [0] + y_order
    sent_y, sent_x = {}, {}
    for s in range(S):
        for d in y_order:
            sent_y[s, d] = send(qbuf.at[s, 0, 0], qbuf.at[s, 0, d], on_y(d))
    sent_gains = {d: send(gb.at[tp], gb.at[tp], on_tp(d)) for d in range(1, 2 * Z)}
    sent_head = {j: send(wh.at[:, 0:128], wh.at[:, j * 128 : (j + 1) * 128], on_pair(j)) for j in (2, 1)}

    def queries_on(s, ways, d):
        for e in ways:
            sent_x[s, e, d] = send(qbuf.at[s, 0, d], qbuf.at[s, e, d], on_x(e))

    for s in range(S):
        queries_on(s, sides, 0)
        for at, d in enumerate(y_order):
            recv(sent_y[s, d], qbuf.at[s, 0, d])
            queries_on(s, sides, d)
            if at >= 2:
                queries_on(s, opposite, y_steps[at - 2])
        for d in y_steps[max(Y - 3, 0) :]:
            queries_on(s, opposite, d)
        if s == 0:
            for copy in local[5:]:
                copy.wait()
            attend_first()
    y_direct = [d for d in y_order if Y < 8 or min(d, Y - d) <= 2]
    sent_proj = {d: send(wo.at[k, y], wo.at[k, y], on_y(d)) for d in reversed(y_direct)}

    def proj_from(d):
        return wo.at[k, lax.rem(y - d + Y, Y)]

    def half_of(ref, first):
        return ref.at[: W // 2] if first else ref.at[W // 2 :]


    def spread_x(numbers, block, slots, s):
        @pl.when(k == s)
        def _():
            slots[x, k] = block[s]
            for e in x_order:
                copy_of(numbers["same", e], block.at[s], slots.at[x, k], on_x(e)).start()

        @pl.when(k != s)
        def _():
            for e in [0] + x_order:
                there = other_core(on_x(e))
                copy_of(numbers["other", e], block.at[s], slots.at[x, k], there).start()

    def numbers_for(block, slots):
        numbers = {}
        for way, steps in (("same", x_order), ("other", [0] + x_order)):
            for e in steps:
                numbers[way, e] = len(started)
                started.append(copy_of(len(started), block.at[0], slots.at[x, k], on_pair(1)))
        return numbers

    def gathered_x(numbers, slots):
        for (way, e), number in numbers.items():
            recv(number, slots.at[lax.rem(x - e + X, X), k if way == "same" else 1 - k])

    sent_resid = numbers_for(resid, rb)
    for s in range(S):
        spread_x(sent_resid, resid, rb, s)

    sent_o, sent_s = {}, {}

    def attend_others(members, s):
        for e in members:
            for d in y_steps:
                recv(sent_x[s, e, d], qbuf.at[s, e, d])
        if members:
            attend(members, s)
        for e in members:
            sent_o[e, s] = send(obuf.at[e, s], xr.at[e, s], on_x(-e))
            sent_s[e, s] = send(ostat.at[e, s], xs.at[e, s], on_x(-e))

    attend([0], 1)
    for s in range(S):
        attend_others(sides, s)
        attend_others(opposite, s)

    for d in y_direct:
        recv(sent_proj[d], proj_from(d))
    if Y == 8:
        for step, d in ((1, 2), (-1, Y - 2)):
            sent_proj[d + step] = send(proj_from(d), proj_from(d), on_y(step))
        for step, d in ((2, 2), (-2, Y - 2)):
            part = (step > 0, Y // 2)
            sent_proj[part] = send(*[half_of(proj_from(d), step > 0)] * 2, on_y(step))

    sent_yo, sent_ys = {}, {}
    for s in range(S):
        for e in x_order:
            recv(sent_o[e, s], xr.at[e, s])
            recv(sent_s[e, s], xs.at[e, s])
        shares, ystat[s] = merge([ostat[0, s]] + [xs[e, s] for e in x_order])
        table = transposed(shares)
        for h in range(heads):
            at = slice(h * HEAD_SIZE, (h + 1) * HEAD_SIZE)
            total = None
            for place, e in enumerate([0] + x_order):
                column = place * heads + h
                part = obuf[0, s, :, at] if e == 0 else xr[e, s, :, at]
                part = part.astype(F32) * table[:group, column : column + 1]
                total = part if total is None else total + part
            yb[s, :, :, at] = total.reshape(Y, R, HEAD_SIZE).astype(BF16)
        for d in y_order:
            sent_yo[d, s] = send(yb.at[s, d], yr.at[s, d], on_y(-d))
            sent_ys[d, s] = send(ystat.at[s], ys.at[s, d], on_y(-d))
    if Y == 8:
        for d in (3, Y - 3):
            recv(sent_proj[d], proj_from(d))
        for first in (True, False):
            recv(sent_proj[first, Y // 2], half_of(proj_from(Y // 2), first))
    sent_proj = send(wo.at[k], wo.at[k], on_pair(1))
    sent_rows = numbers_for(ab, at_x)
    for s in range(S):
        for d in y_order:
            recv(sent_yo[d, s], yr.at[s, d])
            recv(sent_ys[d, s], ys.at[s, d])
        shares, _ = merge([ystat[s]] + [pltpu.roll(ys[s, d], 128 - d * R, 1) for d in y_order])
        table = transposed(shares)
        for h in range(heads):
            at = slice(h * HEAD_SIZE, (h + 1) * HEAD_SIZE)
            total = None
            for place, d in enumerate([0] + y_order):
                column = place * heads + h
                part = yb[s, 0, :, at] if d == 0 else yr[s, d, :, at]
                part = part.astype(F32) * table[:R, column : column + 1]
                total = part if total is None else total + part
            ab[s, :, at] = total.astype(BF16)
        spread_x(sent_rows, ab, at_x, s)

    recv(sent_proj, wo.at[1 - k])
    gathered_x(sent_resid, rb)
    gathered_x(sent_rows, at_x)
    eight, half = R // 2, cols // 2
    attended = jnp.concatenate([at_x[:, c].reshape(X * R, W) for c in range(2)], axis=1)
    width = wo.shape[-1]
    for j in range(cols // W):
        weights = []
        for c in range(2):
            if width < W:
                each = W // width
                weights.append(
                    jnp.concatenate([wo[c, j * each + i] for i in range(each)], axis=1)
                )
            else:
                first = j * W
                weights.append(wo[c, first // width, :, first % width : first % width + W])
        part = jnp.dot(attended, jnp.concatenate(weights, axis=0), preferred_element_type=F32)
        block = x * (cols // W) + j
        mine = (z == block // 2).astype(F32)
        part = part + rb[:, j % 2].reshape(X * R, W).astype(F32) * mine
        own[:, :, j * W : (j + 1) * W] = part.reshape(Z, eight, W)

    summed = own[...]
    zs[...] = jnp.concatenate([summed[:, :, :half], summed[:, :, half:]], axis=1).astype(BF16)
    sent = {d: send(zs.at[lax.rem(z + d, Z)], zr.at[d], on_z(d)) for d in z_order}
    for d in range(1, 2 * Z):
        recv(sent_gains[d], gb.at[lax.rem(tp - d + 2 * Z, 2 * Z)])
    stream = own[z]
    for d in z_order:
        recv(sent[d], zr.at[d])
        both = zr[d].astype(F32)
        stream = stream + jnp.concatenate([both[:eight], both[eight:]], axis=1)
    gains = [gb[x * (cols // W) + j] for j in range(cols // W)]
    scaled = stream * jnp.concatenate(gains, axis=1)
    ex[x, y, zh] = jnp.concatenate([scaled[:, :half], scaled[:, half:]], axis=0).astype(BF16)

    def near(e):
        return lax.rem(zh - e + ZH, ZH)

    def piece(i, d, e):
        return ex.at[lax.rem(x - i + X, X), lax.rem(y - d + Y, Y), near(e)]

    z_steps = [0] + zh_order
    x_first = z_steps[-1]
    under_way, busy = [], {}

    def launch(now, axis, step, i, d, e):
        size = {"x": X, "y": Y, "z": ZH}[axis]
        device = {"x": on_x, "y": on_y, "z": lambda n: on_z(2 * n)}[axis](step)
        number = send(piece(i, d, e), piece(i, d, e), device)
        way = step % size
        way = way if 2 * way <= size else way - size
        link = (axis, way > 0)
        busy[link] = max(now, busy.get(link, 0.0)) + 0.35 * abs(way)
        there = [i, d, e]
        at = "xyz".index(axis)
        there[at] = (there[at] + step) % size
        hops = abs(way) * (2 if axis == "z" else 1)
        heapq.heappush(under_way, (busy[link] + 1.4 + 0.7 * hops, number, tuple(there)))

    def spread_y(now, i, d, e):
        if d == 0:
            for step in y_direct:
                launch(now, "y", step, i, d, e)
        elif Y == 8 and d in (2, Y - 2):
            step = 1 if d == 2 else -1
            launch(now, "y", step, i, d, e)
            if (i + e + (step > 0)) % 2:
                launch(now, "y", 2 * step, i, d, e)

    def arrived(now, i, d, e):
        if e == x_first and i == d == 0:
            for step in x_order:
                launch(now, "x", step, i, d, e)
        elif e != x_first and i == 0:
            for step in sides:
                launch(now, "x", step, i, d, e)
        if e == x_first or i == 0:
            spread_y(now, i, d, e)
        elif X == 4 and i == (1 if (z_steps.index(e) + d) % 2 else X - 1):
            launch(now, "x", 1 if i == 1 else -1, i, d, e)

    for e in zh_order:
        launch(0.0, "z", e, 0, 0, 0)
    arrived(0.0, 0, 0, 0)
    lane = lax.broadcasted_iota(jnp.int32, (eight, 128), 1)
    squares = jnp.sum(stream * stream, -1, keepdims=True)
    wanted = tt[k, pl.ds(pl.multiple_of(parity * eight, eight), eight), :] * (x == zh).astype(F32)
    ea[zh] = jnp.where(lane == 0, squares, jnp.where(lane == 1, wanted, 0.0))
    sent_az = {e: send(ea.at[zh], ea.at[zh], on_z(2 * e)) for e in zh_order}
    recv(sent_head[2], wh.at[:, 256:384])
    sent_head[3] = send(wh.at[:, 256:384], wh.at[:, 384:512], on_pair(1))

    block = ZH * eight
    per_tile = 128 // block
    tiles = xa.shape[1]
    sent_ay, sent_ax = {}, {}

    def rows_along_y():
        for e in zh_order:
            recv(sent_az[e], ea.at[near(e)])
        ya[y] = transposed([ea[i] for i in range(ZH)])[:8]
        for d in y_order:
            sent_ay[d] = send(ya.at[y], ya.at[y], on_y(d))

    def rows_along_x():
        for d in y_order:
            recv(sent_ay[d], ya.at[lax.rem(y - d + Y, Y)])
        for i in range(tiles):
            total = None
            for place in range(min(per_tile, Y)):
                tile = ya[i * per_tile + place]
                if place:
                    tile = pltpu.roll(tile, place * block, 1)
                total = tile if total is None else total + tile
            xa[x, i] = total
        for e in x_order:
            sent_ax[e] = send(xa.at[x], xa.at[x], on_x(e))

    slots = Y * ZH * eight

    def multiply(i, e):
        if not complete:
            for j in (1, 3):
                recv(sent_head[j], wh.at[:, j * 128 : (j + 1) * 128])
        from_x, from_z = lax.rem(x - i + X, X), near(e)
        block = ex[from_x, :, from_z].reshape(Y * R, half)
        total = None
        for upper in range(2):
            start = pl.multiple_of(from_x * cols + upper * half, half)
            part = jnp.dot(block, wh[pl.ds(start, half), :], preferred_element_type=F32)
            part = part.reshape(Y, 2, eight, 4 * 128)[:, upper]
            total = part if total is None else total + part
        if e in complete:
            lg[:, from_z] += total
        else:
            lg[:, from_z] = total
        complete.append(e)

    complete = []
    missing = {(i, e): Y for i in range(X) for e in z_steps}
    missing[0, 0] -= 1
    later = [(6.0, rows_along_y), (11.0, rows_along_x)]
    while under_way:
        now, number, place = heapq.heappop(under_way)
        while later and later[0][0] < now:
            later.pop(0)[1]()
        recv(number, piece(*place))
        arrived(now, *place)
        i, _, e = place
        missing[i, e] -= 1
        if missing[i, e] == 0:
            multiply(i, e)
    for _, step in later:
        step()
    if Y == 1:
        multiply(0, 0)
    for e in x_order:
        recv(sent_ax[e], xa.at[lax.rem(x - e + X, X)])
    span = min(128, slots)
    fin = None
    for i in range(tiles):
        total = xa[0, i]
        for from_x in range(1, X):
            total = total + xa[from_x, i]
        table = transposed([lax.rsqrt(total * (1.0 / (X * cols)) + NORM_EPSILON), total])
        logits = lg[i * per_tile : (i + 1) * per_tile].reshape(span, 4 * 128) * table[:span, 0:1]
        wanted = table[:span, 9:10]
        top = jnp.max(logits, -1, keepdims=True)
        sums = jnp.sum(jnp.exp(logits - top), -1, keepdims=True)
        lane = lax.broadcasted_iota(jnp.int32, (span, 128), 1)
        picked = jnp.zeros((span, 128), F32)
        for j in range(4):
            first = (ctx * (2 * Z) + on_pair(j)[1]) * 128
            hit = (lane + first).astype(F32) == wanted
            picked = picked + jnp.where(hit, logits[:, j * 128 : (j + 1) * 128], 0.0)
        tile = columns_to_tile(
            {i: top + jnp.log(sums), 2 + i: jnp.sum(picked, -1, keepdims=True)}
        )
        fin = tile if fin is None else fin + tile
    ft[tp] = fin[:4]

    row = lax.broadcasted_iota(jnp.int32, (8, 128), 0)

    def combine(parts):
        _, log_sum = merge(parts)
        logs = lax.broadcasted_iota(jnp.int32, parts[0].shape, 0) < parts[0].shape[0] // 2
        return jnp.where(logs, log_sum, functools.reduce(jnp.add, parts))

    sent = {d: send(ft.at[tp], ft.at[tp], on_tp(d)) for d in range(1, 2 * Z)}
    settled = len(started)
    for copy in started:
        copy.wait_send()
    for d in range(1, 2 * Z):
        recv(sent[d], ft.at[lax.rem(tp - d + 2 * Z, 2 * Z)])
    for s in range(S):
        first, second = (
            combine([ft[4 * i + 2 * upper + s] for i in range(ZH)]) for upper in range(2)
        )
        fy[y, s] = jnp.concatenate([first[:2], second[:2], first[2:], second[2:]], axis=0)
    sent = {d: send(fy.at[y], fy.at[y], on_y(d)) for d in y_order}
    for d in y_order:
        recv(sent[d], fy.at[lax.rem(y - d + Y, Y)])
    for s in range(S):
        fx[x, s] = combine([fy[i, s] for i in range(Y)])
    sent = {e: send(fx.at[x], fx.at[x], on_x(e)) for e in x_order}
    for e in x_order:
        recv(sent[e], fx.at[lax.rem(x - e + X, X)])

    lane = lax.broadcasted_iota(jnp.int32, (8, 128), 1)
    from_y = lax.rem(row, 2) * per_tile + lane // block
    from_x = lax.rem(lane, block) // eight
    slot = (from_x * Y + from_y) * R + (row // 2) * eight + lax.rem(lane, eight)
    counted = (row < 4) & (from_y < Y)
    sample_sum, tokens = None, []
    first = lax.rem(y, per_tile) * block + x * eight
    member = lax.broadcasted_iota(jnp.int32, (R, 128), 0)
    place = lax.broadcasted_iota(jnp.int32, (R, 128), 1) == first + lax.rem(member, eight)
    for s in range(S):
        tile = combine([fx[i, s] for i in range(X)])
        tile = tile - pltpu.roll(tile, 4, 0)
        tile = jnp.where(counted & (slot < live_rows[s]), tile, 0.0)
        total = jnp.sum(jnp.sum(tile, 1, keepdims=True), 0, keepdims=True)
        total = total / jnp.full((1, 1), mask_total[s], jnp.int32).astype(F32)
        sample_sum = total if sample_sum is None else sample_sum + total
        in_first = y < per_tile
        lower = jnp.where(in_first, tile[0:1], tile[1:2])
        upper = jnp.where(in_first, tile[2:3], tile[3:4])
        tokens.append(jnp.where(place, jnp.where(member < eight, lower, upper), 0.0))
    loss[...] = sample_sum * (1.0 / S)
    token = jnp.sum(transposed(tokens), 0, keepdims=True)
    for s in range(S):
        out[0, s : s + 1, :] = token[:, s * R : (s + 1) * R]
    finished = [
        pltpu.make_async_copy(out, out_hbm, local_sem.at[0]),
        pltpu.make_async_copy(loss, loss_hbm, local_sem.at[1]),
    ]
    for copy in finished:
        copy.start()
    for copy in started[settled:]:
        copy.wait_send()
    for copy in finished:
        copy.wait()
    assert len(started) == copies(X, Y, Z), len(started)


def copies(X, Y, Z):
    x, y, z, zh = X - 1, Y - 1, Z - 1, Z // 2 - 1
    count = 2 * (y + x + x * y) + 2 + 2 * Z - 1 + (8 if Y == 8 else y) + 2 * (2 * x + 1) + 4 * x + 4 * y + 1 + z
    count += X * Y * Z // 2 - 1 + 1 + zh + y + x
    return count + 2 * Z - 1 + y + x


def on_device(
    sizes,
    queries,
    positions,
    cached_keys,
    cached_values,
    residual_rows,
    out_proj,
    norm_gain,
    head_weight,
    targets,
    live_rows,
    mask_total,
):
    X, Y, Z = sizes
    S, R, W = queries.shape
    L = cached_keys.shape[1]
    D = head_weight.shape[0]
    cols = D // X
    ZH = Z // 2
    block = ZH * (R // 2)
    tiles = -(-Y * block // 128)
    hbm = pl.BlockSpec(memory_space=pl.ANY)
    scratch = [
        ((S, R, W), BF16),
        ((S, R), jnp.int32),
        ((S, R), jnp.int32),
        ((S, R, W), BF16),
        ((W,), BF16),
        ((S, L, W), BF16),
        ((S, L, W), BF16),
        ((S, X, Y, R, W), BF16),
        ((X, S, Y * R, W), BF16),
        ((X, S, W // HEAD_SIZE, 128), F32),
        ((X, S, Y * R, W), BF16),
        ((X, S, W // HEAD_SIZE, 128), F32),
        ((S, Y, R, W), BF16),
        ((S, W // HEAD_SIZE, 128), F32),
        ((S, Y, R, W), BF16),
        ((S, Y, W // HEAD_SIZE, 128), F32),
        ((S, R, W), BF16),
        ((X, 2, R, W), BF16),
        ((X, 2, R, W), BF16),
        ((2 * Z, 1, W), F32),
        ((2, Y, W, out_proj.shape[1]), BF16),
        ((D, 4 * 128), BF16),
        ((Z, R // 2, cols), F32),
        ((S, R, 128), F32),
        ((Z, R, cols // 2), BF16),
        ((Z, R, cols // 2), BF16),
        ((ZH, R // 2, 128), F32),
        ((X, Y, ZH, R, cols // 2), BF16),
        ((Y, 8, 128), F32),
        ((X, tiles, 8, 128), F32),
        ((Y, ZH, R // 2, 4 * 128), F32),
        ((2 * Z, 4, 128), F32),
        ((Y, S, 8, 128), F32),
        ((X, S, 8, 128), F32),
        ((1, S, R), F32),
        ((1, 1), F32),
    ]
    count = copies(X, Y, Z)
    token_nll, loss = pl.pallas_call(
        functools.partial(kernel, sizes),
        out_shape=[jax.ShapeDtypeStruct((1, S, R), F32), jax.ShapeDtypeStruct((1, 1), F32)],
        in_specs=[hbm] * 11,
        out_specs=[hbm, hbm],
        scratch_shapes=[pltpu.SMEM((S,), jnp.int32)] * 2
        + [pltpu.VMEM(*shape) for shape in scratch]
        + [
            pltpu.SemaphoreType.DMA((11,)),
            pltpu.SemaphoreType.DMA((count,)),
            pltpu.SemaphoreType.DMA((count,)),
        ],
        compiler_params=pltpu.CompilerParams(
            collective_id=0, has_side_effects=True, vmem_limit_bytes=60 * 1024 * 1024
        ),
        name="cloze",
    )(
        live_rows, mask_total, queries, positions, targets, residual_rows,
        norm_gain, cached_keys, cached_values, out_proj, head_weight,
    )
    return (token_nll.reshape(S, R), loss.reshape(()))


def solution(mesh):
    Z = mesh.shape["tp"] // 2
    X = Z // 2
    sizes = (X, mesh.shape["ctx"] // X, Z)
    in_specs = (
        P(None, "ctx", "tp"),
        P(None, "ctx"),
        P(None, "ctx", "tp"),
        P(None, "ctx", "tp"),
        P(None, "ctx", "tp"),
        P("tp", "ctx"),
        P("tp"),
        P(None, ("ctx", "tp")),
        P(None, "ctx"),
        P(),
        P(),
    )
    return jax.shard_map(
        functools.partial(on_device, sizes),
        mesh=mesh,
        in_specs=in_specs,
        out_specs=(P(None, "ctx"), P()),
        check_vma=False,
    )
```

```python
import functools
import heapq
import math

import jax
import jax.numpy as jnp
from jax import lax
from jax.experimental import pallas as pl
from jax.experimental.pallas import tpu as pltpu
from jax.sharding import PartitionSpec as P

HEAD_SIZE = 128
ROPE_BASE = 500000.0
NORM_EPSILON = 1e-05
F32 = jnp.float32
BF16 = jnp.bfloat16


def near_first(n):
    return sorted(range(1, n), key=lambda d: (min(d, n - d), d))


def transposed(tiles):
    stacked = jnp.concatenate(tiles, axis=0)
    if stacked.shape[0] < 128:
        stacked = jnp.concatenate(
            [stacked, jnp.zeros((128 - stacked.shape[0], 128), F32)], axis=0
        )
    return stacked.T


def columns_to_tile(columns):
    rows = next(iter(columns.values())).shape[0]
    lane = lax.broadcasted_iota(jnp.int32, (rows, 128), 1)
    table = jnp.zeros((rows, 128), F32)
    for at, column in columns.items():
        table = jnp.where(lane == at, column, table)
    if rows < 128:
        table = jnp.concatenate([table, jnp.zeros((128 - rows, 128), F32)], axis=0)
    return table.T[:8]


def merge(tiles):
    top = functools.reduce(jnp.maximum, tiles)
    weights = [jnp.exp(tile - top) for tile in tiles]
    total = functools.reduce(jnp.add, weights)
    return [weight / total for weight in weights], top + jnp.log(total)


def kernel(
    sizes,
    live_hbm, mask_hbm, q_hbm, positions_hbm, targets_hbm, resid_hbm, gain_hbm,
    keys_hbm, values_hbm, proj_hbm, head_hbm,
    out_hbm, loss_hbm,
    live_rows, mask_total, q, positions, targets, resid, gain, keys, values, qbuf, obuf, ostat,
    xr, xs, yb, ystat, yr, ys, ab, at_x, rb, gb, wo, wh, own, tt, zs, zr, ea, ex, ya, xa, lg, ft, fy, fx, out, loss,
    local_sem, send_sem, recv_sem,
):
    X, Y, Z = sizes
    S, R, W = q_hbm.shape
    heads = W // HEAD_SIZE
    ZH = Z // 2
    cols = own.shape[-1]
    ctx, tp = lax.axis_index("ctx"), lax.axis_index("tp")
    x, y = ctx // Y, lax.rem(ctx, Y)
    z, k = tp // 2, lax.rem(tp, 2)
    zh, parity = z // 2, lax.rem(z, 2)
    z_other = z + 1 - 2 * parity

    def on_x(d):
        return (lax.rem(x + d + X, X) * Y + y, tp)

    def on_y(d):
        return (x * Y + lax.rem(y + d + Y, Y), tp)

    def on_z(d):
        return (ctx, lax.rem(z + d + Z, Z) * 2 + k)

    def on_pair(j):
        return (ctx, (z_other if j >= 2 else z) * 2 + (1 - k if j % 2 else k))

    started = []

    def copy_of(i, src, dst, device):
        return pltpu.make_async_remote_copy(
            src_ref=src,
            dst_ref=dst,
            send_sem=send_sem.at[i],
            recv_sem=recv_sem.at[i],
            device_id=device,
            device_id_type=pl.DeviceIdType.MESH,
        )

    def send(src, dst, device):
        copy = copy_of(len(started), src, dst, device)
        copy.start()
        started.append(copy)
        return len(started) - 1

    def recv(i, dst):
        copy_of(i, dst, dst, on_pair(1)).wait_recv()

    def on_tp(d):
        return (ctx, lax.rem(tp + d, 2 * Z))

    def other_core(device):
        return (device[0], z * 2 + 1 - k)

    x_order, y_order, z_order = near_first(X), near_first(Y), near_first(Z)
    zh_order = near_first(ZH)

    fetched = [
        (positions_hbm, positions), (q_hbm, q),
        (head_hbm, wh.at[:, 0:128]), (targets_hbm, targets), (gain_hbm, gain),
        (live_hbm, live_rows), (mask_hbm, mask_total),
        (resid_hbm, resid), (keys_hbm, keys), (values_hbm, values), (proj_hbm, wo.at[k, y]),
    ]
    local = [
        pltpu.make_async_copy(src, dst, local_sem.at[i]) for i, (src, dst) in enumerate(fetched)
    ]
    for copy in local:
        copy.start()

    barrier = pltpu.get_barrier_semaphore()
    peers = [on_y(d) for d in y_order] + [on_x(d) for d in x_order]
    peers += [on_tp(d) for d in range(1, 2 * Z)]
    peers += [other_core(on_x(d)) for d in x_order]
    for peer in peers:
        pl.semaphore_signal(
            barrier, inc=1, device_id=peer, device_id_type=pl.DeviceIdType.MESH
        )

    def column_table(ref):
        table = jnp.concatenate([ref[...].astype(F32), jnp.zeros((S, 128 - R), F32)], axis=1)
        return transposed([jnp.concatenate([table, jnp.zeros((8 - S, 128), F32)], axis=0)])

    lane = lax.broadcasted_iota(jnp.int32, (R, HEAD_SIZE), 1)
    place = lax.rem(lane, HEAD_SIZE // 2).astype(F32)
    frequency = ROPE_BASE ** (-2.0 * place / HEAD_SIZE)
    local[0].wait()
    places = column_table(positions)
    angles = [places[:R, s : s + 1] * frequency for s in range(S)]
    turns = [(jnp.cos(angle), jnp.sin(angle)) for angle in angles]
    local[1].wait()
    for s in range(S):
        cosine, sine = turns[s]
        sine = jnp.where(lane < HEAD_SIZE // 2, -sine, sine)
        for h in range(heads):
            at = slice(h * HEAD_SIZE, (h + 1) * HEAD_SIZE)
            part = q[s, :, at].astype(F32)
            turned = part * cosine + pltpu.roll(part, HEAD_SIZE // 2, 1) * sine
            qbuf[s, 0, 0, :, at] = turned.astype(BF16)
    for copy in local[2:5]:
        copy.wait()
    gb[tp] = gain[...].astype(F32).reshape(1, W)
    wanted = column_table(targets)
    for s in range(S):
        tt[s] = jnp.broadcast_to(wanted[:R, s : s + 1], (R, 128))
    pl.semaphore_wait(barrier, len(peers))

    scale = math.log2(math.e) / math.sqrt(HEAD_SIZE)
    group = Y * R

    def attend(members, s):
        logs = [{} for _ in members]
        for h in range(heads):
            at = slice(h * HEAD_SIZE, (h + 1) * HEAD_SIZE)
            block = [qbuf[s, e, :, :, at].reshape(group, HEAD_SIZE) for e in members]
            scores = lax.dot_general(
                jnp.concatenate(block, axis=0),
                keys[s, :, at],
                (((1,), (1,)), ((), ())),
                preferred_element_type=F32,
            )
            top = jnp.max(scores, -1, keepdims=True)
            weights = jnp.exp2((scores - top) * scale)
            total = jnp.sum(weights, -1, keepdims=True)
            summed = jnp.dot(
                weights.astype(BF16), values[s, :, at], preferred_element_type=F32
            )
            summed = (summed / total).astype(BF16)
            log_sum = top * (1.0 / math.sqrt(HEAD_SIZE)) + jnp.log(total)
            for place, e in enumerate(members):
                rows = slice(place * group, (place + 1) * group)
                obuf[e, s, :, at] = summed[rows]
                logs[place][h] = log_sum[rows]
        for place, e in enumerate(members):
            ostat[e, s] = columns_to_tile(logs[place])[:heads]

    def attend_first():
        attend([0], 0)

    sides = {1: [], 2: [1]}.get(X, [1, X - 1])
    opposite, y_steps = x_order[len(sides) :], [0] + y_order
    sent_y, sent_x = {}, {}
    for s in range(S):
        for d in y_order:
            sent_y[s, d] = send(qbuf.at[s, 0, 0], qbuf.at[s, 0, d], on_y(d))
    sent_gains = {d: send(gb.at[tp], gb.at[tp], on_tp(d)) for d in range(1, 2 * Z)}
    sent_head = {j: send(wh.at[:, 0:128], wh.at[:, j * 128 : (j + 1) * 128], on_pair(j)) for j in (2, 1)}

    def queries_on(s, ways, d):
        for e in ways:
            sent_x[s, e, d] = send(qbuf.at[s, 0, d], qbuf.at[s, e, d], on_x(e))

    for s in range(S):
        queries_on(s, sides, 0)
        for at, d in enumerate(y_order):
            recv(sent_y[s, d], qbuf.at[s, 0, d])
            queries_on(s, sides, d)
            if at >= 2:
                queries_on(s, opposite, y_steps[at - 2])
        for d in y_steps[max(Y - 3, 0) :]:
            queries_on(s, opposite, d)
        if s == 0:
            for copy in local[5:]:
                copy.wait()
            attend_first()
    y_direct = [d for d in y_order if Y < 8 or min(d, Y - d) <= 2]
    sent_proj = {d: send(wo.at[k, y], wo.at[k, y], on_y(d)) for d in reversed(y_direct)}

    def proj_from(d):
        return wo.at[k, lax.rem(y - d + Y, Y)]

    def half_of(ref, first):
        return ref.at[: W // 2] if first else ref.at[W // 2 :]


    def spread_x(numbers, block, slots, s):
        @pl.when(k == s)
        def _():
            slots[x, k] = block[s]
            for e in x_order:
                copy_of(numbers["same", e], block.at[s], slots.at[x, k], on_x(e)).start()

        @pl.when(k != s)
        def _():
            for e in [0] + x_order:
                there = other_core(on_x(e))
                copy_of(numbers["other", e], block.at[s], slots.at[x, k], there).start()

    def numbers_for(block, slots):
        numbers = {}
        for way, steps in (("same", x_order), ("other", [0] + x_order)):
            for e in steps:
                numbers[way, e] = len(started)
                started.append(copy_of(len(started), block.at[0], slots.at[x, k], on_pair(1)))
        return numbers

    def gathered_x(numbers, slots):
        for (way, e), number in numbers.items():
            recv(number, slots.at[lax.rem(x - e + X, X), k if way == "same" else 1 - k])

    sent_resid = numbers_for(resid, rb)
    for s in range(S):
        spread_x(sent_resid, resid, rb, s)

    sent_o, sent_s = {}, {}

    def attend_others(members, s):
        for e in members:
            for d in y_steps:
                recv(sent_x[s, e, d], qbuf.at[s, e, d])
        if members:
            attend(members, s)
        for e in members:
            sent_o[e, s] = send(obuf.at[e, s], xr.at[e, s], on_x(-e))
            sent_s[e, s] = send(ostat.at[e, s], xs.at[e, s], on_x(-e))

    attend([0], 1)
    for s in range(S):
        attend_others(sides, s)
        attend_others(opposite, s)

    for d in y_direct:
        recv(sent_proj[d], proj_from(d))
    if Y == 8:
        for step, d in ((1, 2), (-1, Y - 2)):
            sent_proj[d + step] = send(proj_from(d), proj_from(d), on_y(step))
        for step, d in ((2, 2), (-2, Y - 2)):
            part = (step > 0, Y // 2)
            sent_proj[part] = send(*[half_of(proj_from(d), step > 0)] * 2, on_y(step))

    sent_yo, sent_ys = {}, {}
    for s in range(S):
        for e in x_order:
            recv(sent_o[e, s], xr.at[e, s])
            recv(sent_s[e, s], xs.at[e, s])
        shares, ystat[s] = merge([ostat[0, s]] + [xs[e, s] for e in x_order])
        table = transposed(shares)
        for h in range(heads):
            at = slice(h * HEAD_SIZE, (h + 1) * HEAD_SIZE)
            total = None
            for place, e in enumerate([0] + x_order):
                column = place * heads + h
                part = obuf[0, s, :, at] if e == 0 else xr[e, s, :, at]
                part = part.astype(F32) * table[:group, column : column + 1]
                total = part if total is None else total + part
            yb[s, :, :, at] = total.reshape(Y, R, HEAD_SIZE).astype(BF16)
        for d in y_order:
            sent_yo[d, s] = send(yb.at[s, d], yr.at[s, d], on_y(-d))
            sent_ys[d, s] = send(ystat.at[s], ys.at[s, d], on_y(-d))
    if Y == 8:
        for d in (3, Y - 3):
            recv(sent_proj[d], proj_from(d))
        for first in (True, False):
            recv(sent_proj[first, Y // 2], half_of(proj_from(Y // 2), first))
    sent_proj = send(wo.at[k], wo.at[k], on_pair(1))
    sent_rows = numbers_for(ab, at_x)
    for s in range(S):
        for d in y_order:
            recv(sent_yo[d, s], yr.at[s, d])
            recv(sent_ys[d, s], ys.at[s, d])
        shares, _ = merge([ystat[s]] + [pltpu.roll(ys[s, d], 128 - d * R, 1) for d in y_order])
        table = transposed(shares)
        for h in range(heads):
            at = slice(h * HEAD_SIZE, (h + 1) * HEAD_SIZE)
            total = None
            for place, d in enumerate([0] + y_order):
                column = place * heads + h
                part = yb[s, 0, :, at] if d == 0 else yr[s, d, :, at]
                part = part.astype(F32) * table[:R, column : column + 1]
                total = part if total is None else total + part
            ab[s, :, at] = total.astype(BF16)
        spread_x(sent_rows, ab, at_x, s)

    recv(sent_proj, wo.at[1 - k])
    gathered_x(sent_resid, rb)
    gathered_x(sent_rows, at_x)
    eight, half = R // 2, cols // 2
    attended = jnp.concatenate([at_x[:, c].reshape(X * R, W) for c in range(2)], axis=1)
    width = wo.shape[-1]
    for j in range(cols // W):
        weights = []
        for c in range(2):
            if width < W:
                each = W // width
                weights.append(
                    jnp.concatenate([wo[c, j * each + i] for i in range(each)], axis=1)
                )
            else:
                first = j * W
                weights.append(wo[c, first // width, :, first % width : first % width + W])
        part = jnp.dot(attended, jnp.concatenate(weights, axis=0), preferred_element_type=F32)
        block = x * (cols // W) + j
        mine = (z == block // 2).astype(F32)
        part = part + rb[:, j % 2].reshape(X * R, W).astype(F32) * mine
        own[:, :, j * W : (j + 1) * W] = part.reshape(Z, eight, W)

    summed = own[...]
    zs[...] = jnp.concatenate([summed[:, :, :half], summed[:, :, half:]], axis=1).astype(BF16)
    sent = {d: send(zs.at[lax.rem(z + d, Z)], zr.at[d], on_z(d)) for d in z_order}
    for d in range(1, 2 * Z):
        recv(sent_gains[d], gb.at[lax.rem(tp - d + 2 * Z, 2 * Z)])
    stream = own[z]
    for d in z_order:
        recv(sent[d], zr.at[d])
        both = zr[d].astype(F32)
        stream = stream + jnp.concatenate([both[:eight], both[eight:]], axis=1)
    gains = [gb[x * (cols // W) + j] for j in range(cols // W)]
    scaled = stream * jnp.concatenate(gains, axis=1)
    ex[x, y, zh] = jnp.concatenate([scaled[:, :half], scaled[:, half:]], axis=0).astype(BF16)

    def near(e):
        return lax.rem(zh - e + ZH, ZH)

    def piece(i, d, e):
        return ex.at[lax.rem(x - i + X, X), lax.rem(y - d + Y, Y), near(e)]

    z_steps = [0] + zh_order
    x_first = z_steps[-1]
    under_way, busy = [], {}

    opposite_numbers = {}

    def launch_opposite(core, now, step, i, d, e):
        if (d, e) not in opposite_numbers:
            opposite_numbers[d, e] = len(started)
            started.append(copy_of(len(started), piece(i, d, e), piece(i, d, e), on_x(step)))

        @pl.when(k == core)
        def _():
            copy_of(opposite_numbers[d, e], piece(i, d, e), piece(i, d, e), on_x(step)).start()

        if core == 1:
            number = opposite_numbers[d, e]
            heapq.heappush(under_way, (now + 2.5, number, (2, d, e)))

    def launch(now, axis, step, i, d, e):
        size = {"x": X, "y": Y, "z": ZH}[axis]
        device = {"x": on_x, "y": on_y, "z": lambda n: on_z(2 * n)}[axis](step)
        number = send(piece(i, d, e), piece(i, d, e), device)
        way = step % size
        way = way if 2 * way <= size else way - size
        link = (axis, way > 0)
        busy[link] = max(now, busy.get(link, 0.0)) + 0.35 * abs(way)
        there = [i, d, e]
        at = "xyz".index(axis)
        there[at] = (there[at] + step) % size
        hops = abs(way) * (2 if axis == "z" else 1)
        heapq.heappush(under_way, (busy[link] + 1.4 + 0.7 * hops, number, tuple(there)))

    def spread_y(now, i, d, e):
        if d == 0:
            for step in y_direct:
                launch(now, "y", step, i, d, e)
        elif Y == 8 and d in (2, Y - 2):
            step = 1 if d == 2 else -1
            launch(now, "y", step, i, d, e)
            if (i + e + (step > 0)) % 2:
                launch(now, "y", 2 * step, i, d, e)

    def arrived(now, i, d, e):
        if e == x_first and i == d == 0:
            for step in x_order:
                launch(now, "x", step, i, d, e)
        elif e != x_first and i == 0:
            for step in sides:
                launch(now, "x", step, i, d, e)
            if X == 4 and Y == 8 and d not in [0] + y_direct:
                launch_opposite(0, now, 2, i, d, e)
        if e == x_first or i == 0:
            spread_y(now, i, d, e)
        elif X == 4 and i == (1 if (z_steps.index(e) + d) % 2 else X - 1):
            if d in [0] + y_direct:
                launch(now, "x", 1 if i == 1 else -1, i, d, e)
            else:
                launch_opposite(1, now, 1 if i == 1 else -1, i, d, e)

    for e in zh_order:
        launch(0.0, "z", e, 0, 0, 0)
    arrived(0.0, 0, 0, 0)
    lane = lax.broadcasted_iota(jnp.int32, (eight, 128), 1)
    squares = jnp.sum(stream * stream, -1, keepdims=True)
    wanted = tt[k, pl.ds(pl.multiple_of(parity * eight, eight), eight), :] * (x == zh).astype(F32)
    ea[zh] = jnp.where(lane == 0, squares, jnp.where(lane == 1, wanted, 0.0))
    sent_az = {e: send(ea.at[zh], ea.at[zh], on_z(2 * e)) for e in zh_order}
    recv(sent_head[2], wh.at[:, 256:384])
    sent_head[3] = send(wh.at[:, 256:384], wh.at[:, 384:512], on_pair(1))

    block = ZH * eight
    per_tile = 128 // block
    tiles = xa.shape[1]
    sent_ay, sent_ax = {}, {}

    def rows_along_y():
        for e in zh_order:
            recv(sent_az[e], ea.at[near(e)])
        ya[y] = transposed([ea[i] for i in range(ZH)])[:8]
        for d in y_order:
            sent_ay[d] = send(ya.at[y], ya.at[y], on_y(d))

    def rows_along_x():
        for d in y_order:
            recv(sent_ay[d], ya.at[lax.rem(y - d + Y, Y)])
        for i in range(tiles):
            total = None
            for place in range(min(per_tile, Y)):
                tile = ya[i * per_tile + place]
                if place:
                    tile = pltpu.roll(tile, place * block, 1)
                total = tile if total is None else total + tile
            xa[x, i] = total
        for e in x_order:
            sent_ax[e] = send(xa.at[x], xa.at[x], on_x(e))

    slots = Y * ZH * eight

    def multiply(i, e):
        if not complete:
            for j in (1, 3):
                recv(sent_head[j], wh.at[:, j * 128 : (j + 1) * 128])
        from_x, from_z = lax.rem(x - i + X, X), near(e)
        block = ex[from_x, :, from_z].reshape(Y * R, half)
        total = None
        for upper in range(2):
            start = pl.multiple_of(from_x * cols + upper * half, half)
            part = jnp.dot(block, wh[pl.ds(start, half), :], preferred_element_type=F32)
            part = part.reshape(Y, 2, eight, 4 * 128)[:, upper]
            total = part if total is None else total + part
        if e in complete:
            lg[:, from_z] += total
        else:
            lg[:, from_z] = total
        complete.append(e)

    complete = []
    missing = {(i, e): Y for i in range(X) for e in z_steps}
    missing[0, 0] -= 1
    later = [(6.0, rows_along_y), (11.0, rows_along_x)]
    while under_way:
        now, number, place = heapq.heappop(under_way)
        while later and later[0][0] < now:
            later.pop(0)[1]()
        recv(number, piece(*place))
        arrived(now, *place)
        i, _, e = place
        missing[i, e] -= 1
        if missing[i, e] == 0:
            multiply(i, e)
    for _, step in later:
        step()
    if Y == 1:
        multiply(0, 0)
    for e in x_order:
        recv(sent_ax[e], xa.at[lax.rem(x - e + X, X)])
    span = min(128, slots)
    fin = None
    for i in range(tiles):
        total = xa[0, i]
        for from_x in range(1, X):
            total = total + xa[from_x, i]
        table = transposed([lax.rsqrt(total * (1.0 / (X * cols)) + NORM_EPSILON), total])
        logits = lg[i * per_tile : (i + 1) * per_tile].reshape(span, 4 * 128) * table[:span, 0:1]
        wanted = table[:span, 9:10]
        top = jnp.max(logits, -1, keepdims=True)
        sums = jnp.sum(jnp.exp(logits - top), -1, keepdims=True)
        lane = lax.broadcasted_iota(jnp.int32, (span, 128), 1)
        picked = jnp.zeros((span, 128), F32)
        for j in range(4):
            first = (ctx * (2 * Z) + on_pair(j)[1]) * 128
            hit = (lane + first).astype(F32) == wanted
            picked = picked + jnp.where(hit, logits[:, j * 128 : (j + 1) * 128], 0.0)
        tile = columns_to_tile(
            {i: top + jnp.log(sums), 2 + i: jnp.sum(picked, -1, keepdims=True)}
        )
        fin = tile if fin is None else fin + tile
    ft[tp] = fin[:4]

    row = lax.broadcasted_iota(jnp.int32, (8, 128), 0)

    def combine(parts):
        _, log_sum = merge(parts)
        logs = lax.broadcasted_iota(jnp.int32, parts[0].shape, 0) < parts[0].shape[0] // 2
        return jnp.where(logs, log_sum, functools.reduce(jnp.add, parts))

    sent = {d: send(ft.at[tp], ft.at[tp], on_tp(d)) for d in range(1, 2 * Z)}
    settled = len(started)
    for copy in started:
        copy.wait_send()
    for d in range(1, 2 * Z):
        recv(sent[d], ft.at[lax.rem(tp - d + 2 * Z, 2 * Z)])
    for s in range(S):
        first, second = (
            combine([ft[4 * i + 2 * upper + s] for i in range(ZH)]) for upper in range(2)
        )
        fy[y, s] = jnp.concatenate([first[:2], second[:2], first[2:], second[2:]], axis=0)
    sent = {d: send(fy.at[y], fy.at[y], on_y(d)) for d in y_order}
    for d in y_order:
        recv(sent[d], fy.at[lax.rem(y - d + Y, Y)])
    for s in range(S):
        fx[x, s] = combine([fy[i, s] for i in range(Y)])
    sent = {e: send(fx.at[x], fx.at[x], on_x(e)) for e in x_order}
    for e in x_order:
        recv(sent[e], fx.at[lax.rem(x - e + X, X)])

    lane = lax.broadcasted_iota(jnp.int32, (8, 128), 1)
    from_y = lax.rem(row, 2) * per_tile + lane // block
    from_x = lax.rem(lane, block) // eight
    slot = (from_x * Y + from_y) * R + (row // 2) * eight + lax.rem(lane, eight)
    counted = (row < 4) & (from_y < Y)
    sample_sum, tokens = None, []
    first = lax.rem(y, per_tile) * block + x * eight
    member = lax.broadcasted_iota(jnp.int32, (R, 128), 0)
    place = lax.broadcasted_iota(jnp.int32, (R, 128), 1) == first + lax.rem(member, eight)
    for s in range(S):
        tile = combine([fx[i, s] for i in range(X)])
        tile = tile - pltpu.roll(tile, 4, 0)
        tile = jnp.where(counted & (slot < live_rows[s]), tile, 0.0)
        total = jnp.sum(jnp.sum(tile, 1, keepdims=True), 0, keepdims=True)
        total = total / jnp.full((1, 1), mask_total[s], jnp.int32).astype(F32)
        sample_sum = total if sample_sum is None else sample_sum + total
        in_first = y < per_tile
        lower = jnp.where(in_first, tile[0:1], tile[1:2])
        upper = jnp.where(in_first, tile[2:3], tile[3:4])
        tokens.append(jnp.where(place, jnp.where(member < eight, lower, upper), 0.0))
    loss[...] = sample_sum * (1.0 / S)
    token = jnp.sum(transposed(tokens), 0, keepdims=True)
    for s in range(S):
        out[0, s : s + 1, :] = token[:, s * R : (s + 1) * R]
    finished = [
        pltpu.make_async_copy(out, out_hbm, local_sem.at[0]),
        pltpu.make_async_copy(loss, loss_hbm, local_sem.at[1]),
    ]
    for copy in finished:
        copy.start()
    for copy in started[settled:]:
        copy.wait_send()
    for copy in finished:
        copy.wait()
    assert len(started) == copies(X, Y, Z), len(started)


def copies(X, Y, Z):
    x, y, z, zh = X - 1, Y - 1, Z - 1, Z // 2 - 1
    count = 2 * (y + x + x * y) + 2 + 2 * Z - 1 + (8 if Y == 8 else y) + 2 * (2 * x + 1) + 4 * x + 4 * y + 1 + z
    count += X * Y * Z // 2 - 1 + 1 + zh + y + x
    return count + 2 * Z - 1 + y + x


def on_device(
    sizes,
    queries,
    positions,
    cached_keys,
    cached_values,
    residual_rows,
    out_proj,
    norm_gain,
    head_weight,
    targets,
    live_rows,
    mask_total,
):
    X, Y, Z = sizes
    S, R, W = queries.shape
    L = cached_keys.shape[1]
    D = head_weight.shape[0]
    cols = D // X
    ZH = Z // 2
    block = ZH * (R // 2)
    tiles = -(-Y * block // 128)
    hbm = pl.BlockSpec(memory_space=pl.ANY)
    scratch = [
        ((S, R, W), BF16),
        ((S, R), jnp.int32),
        ((S, R), jnp.int32),
        ((S, R, W), BF16),
        ((W,), BF16),
        ((S, L, W), BF16),
        ((S, L, W), BF16),
        ((S, X, Y, R, W), BF16),
        ((X, S, Y * R, W), BF16),
        ((X, S, W // HEAD_SIZE, 128), F32),
        ((X, S, Y * R, W), BF16),
        ((X, S, W // HEAD_SIZE, 128), F32),
        ((S, Y, R, W), BF16),
        ((S, W // HEAD_SIZE, 128), F32),
        ((S, Y, R, W), BF16),
        ((S, Y, W // HEAD_SIZE, 128), F32),
        ((S, R, W), BF16),
        ((X, 2, R, W), BF16),
        ((X, 2, R, W), BF16),
        ((2 * Z, 1, W), F32),
        ((2, Y, W, out_proj.shape[1]), BF16),
        ((D, 4 * 128), BF16),
        ((Z, R // 2, cols), F32),
        ((S, R, 128), F32),
        ((Z, R, cols // 2), BF16),
        ((Z, R, cols // 2), BF16),
        ((ZH, R // 2, 128), F32),
        ((X, Y, ZH, R, cols // 2), BF16),
        ((Y, 8, 128), F32),
        ((X, tiles, 8, 128), F32),
        ((Y, ZH, R // 2, 4 * 128), F32),
        ((2 * Z, 4, 128), F32),
        ((Y, S, 8, 128), F32),
        ((X, S, 8, 128), F32),
        ((1, S, R), F32),
        ((1, 1), F32),
    ]
    count = copies(X, Y, Z)
    token_nll, loss = pl.pallas_call(
        functools.partial(kernel, sizes),
        out_shape=[jax.ShapeDtypeStruct((1, S, R), F32), jax.ShapeDtypeStruct((1, 1), F32)],
        in_specs=[hbm] * 11,
        out_specs=[hbm, hbm],
        scratch_shapes=[pltpu.SMEM((S,), jnp.int32)] * 2
        + [pltpu.VMEM(*shape) for shape in scratch]
        + [
            pltpu.SemaphoreType.DMA((11,)),
            pltpu.SemaphoreType.DMA((count,)),
            pltpu.SemaphoreType.DMA((count,)),
        ],
        compiler_params=pltpu.CompilerParams(
            collective_id=0, has_side_effects=True, vmem_limit_bytes=60 * 1024 * 1024
        ),
        name="cloze",
    )(
        live_rows, mask_total, queries, positions, targets, residual_rows,
        norm_gain, cached_keys, cached_values, out_proj, head_weight,
    )
    return (token_nll.reshape(S, R), loss.reshape(()))


def solution(mesh):
    Z = mesh.shape["tp"] // 2
    X = Z // 2
    sizes = (X, mesh.shape["ctx"] // X, Z)
    in_specs = (
        P(None, "ctx", "tp"),
        P(None, "ctx"),
        P(None, "ctx", "tp"),
        P(None, "ctx", "tp"),
        P(None, "ctx", "tp"),
        P("tp", "ctx"),
        P("tp"),
        P(None, ("ctx", "tp")),
        P(None, "ctx"),
        P(),
        P(),
    )
    return jax.shard_map(
        functools.partial(on_device, sizes),
        mesh=mesh,
        in_specs=in_specs,
        out_specs=(P(None, "ctx"), P()),
        check_vma=False,
    )
```

```python
import functools
import heapq
import math

import jax
import jax.numpy as jnp
from jax import lax
from jax.experimental import pallas as pl
from jax.experimental.pallas import tpu as pltpu
from jax.sharding import PartitionSpec as P

HEAD_SIZE = 128
ROPE_BASE = 500000.0
NORM_EPSILON = 1e-05
F32 = jnp.float32
BF16 = jnp.bfloat16


def near_first(n):
    return sorted(range(1, n), key=lambda d: (min(d, n - d), d))


def transposed(tiles):
    stacked = jnp.concatenate(tiles, axis=0)
    if stacked.shape[0] < 128:
        stacked = jnp.concatenate(
            [stacked, jnp.zeros((128 - stacked.shape[0], 128), F32)], axis=0
        )
    return stacked.T


def columns_to_tile(columns):
    rows = next(iter(columns.values())).shape[0]
    lane = lax.broadcasted_iota(jnp.int32, (rows, 128), 1)
    table = jnp.zeros((rows, 128), F32)
    for at, column in columns.items():
        table = jnp.where(lane == at, column, table)
    if rows < 128:
        table = jnp.concatenate([table, jnp.zeros((128 - rows, 128), F32)], axis=0)
    return table.T[:8]


def merge(tiles):
    top = functools.reduce(jnp.maximum, tiles)
    weights = [jnp.exp(tile - top) for tile in tiles]
    total = functools.reduce(jnp.add, weights)
    return [weight / total for weight in weights], top + jnp.log(total)


def kernel(
    sizes,
    live_hbm, mask_hbm, q_hbm, positions_hbm, targets_hbm, resid_hbm, gain_hbm,
    keys_hbm, values_hbm, proj_hbm, head_hbm,
    out_hbm, loss_hbm,
    live_rows, mask_total, q, positions, targets, resid, gain, keys, values, qbuf, obuf, ostat,
    xr, xs, yb, ystat, yr, ys, ab, at_x, rb, gb, wo, wh, own, tt, zs, zr, ea, ex, ya, xa, lg, ft, fy, fx, out, loss,
    local_sem, send_sem, recv_sem,
):
    X, Y, Z = sizes
    S, R, W = q_hbm.shape
    heads = W // HEAD_SIZE
    ZH = Z // 2
    cols = own.shape[-1]
    ctx, tp = lax.axis_index("ctx"), lax.axis_index("tp")
    x, y = ctx // Y, lax.rem(ctx, Y)
    z, k = tp // 2, lax.rem(tp, 2)
    zh, parity = z // 2, lax.rem(z, 2)
    z_other = z + 1 - 2 * parity

    def on_x(d):
        return (lax.rem(x + d + X, X) * Y + y, tp)

    def on_y(d):
        return (x * Y + lax.rem(y + d + Y, Y), tp)

    def on_z(d):
        return (ctx, lax.rem(z + d + Z, Z) * 2 + k)

    def on_pair(j):
        return (ctx, (z_other if j >= 2 else z) * 2 + (1 - k if j % 2 else k))

    started = []

    def copy_of(i, src, dst, device):
        return pltpu.make_async_remote_copy(
            src_ref=src,
            dst_ref=dst,
            send_sem=send_sem.at[i],
            recv_sem=recv_sem.at[i],
            device_id=device,
            device_id_type=pl.DeviceIdType.MESH,
        )

    def send(src, dst, device):
        copy = copy_of(len(started), src, dst, device)
        copy.start()
        started.append(copy)
        return len(started) - 1

    def recv(i, dst):
        copy_of(i, dst, dst, on_pair(1)).wait_recv()

    def on_tp(d):
        return (ctx, lax.rem(tp + d, 2 * Z))

    def other_core(device):
        return (device[0], z * 2 + 1 - k)

    x_order, y_order, z_order = near_first(X), near_first(Y), near_first(Z)
    zh_order = near_first(ZH)

    fetched = [
        (positions_hbm, positions), (q_hbm, q),
        (head_hbm, wh.at[:, 0:128]), (targets_hbm, targets), (gain_hbm, gain),
        (live_hbm, live_rows), (mask_hbm, mask_total),
        (resid_hbm, resid), (keys_hbm, keys), (values_hbm, values), (proj_hbm, wo.at[k, y]),
    ]
    local = [
        pltpu.make_async_copy(src, dst, local_sem.at[i]) for i, (src, dst) in enumerate(fetched)
    ]
    for copy in local:
        copy.start()

    barrier = pltpu.get_barrier_semaphore()
    peers = [on_y(d) for d in y_order] + [on_x(d) for d in x_order]
    peers += [on_tp(d) for d in range(1, 2 * Z)]
    peers += [other_core(on_x(d)) for d in x_order]
    for peer in peers:
        pl.semaphore_signal(
            barrier, inc=1, device_id=peer, device_id_type=pl.DeviceIdType.MESH
        )

    def column_table(ref):
        table = jnp.concatenate([ref[...].astype(F32), jnp.zeros((S, 128 - R), F32)], axis=1)
        return transposed([jnp.concatenate([table, jnp.zeros((8 - S, 128), F32)], axis=0)])

    lane = lax.broadcasted_iota(jnp.int32, (R, HEAD_SIZE), 1)
    place = lax.rem(lane, HEAD_SIZE // 2).astype(F32)
    frequency = ROPE_BASE ** (-2.0 * place / HEAD_SIZE)
    local[0].wait()
    places = column_table(positions)
    angles = [places[:R, s : s + 1] * frequency for s in range(S)]
    turns = [(jnp.cos(angle), jnp.sin(angle)) for angle in angles]
    local[1].wait()
    for s in range(S):
        cosine, sine = turns[s]
        sine = jnp.where(lane < HEAD_SIZE // 2, -sine, sine)
        for h in range(heads):
            at = slice(h * HEAD_SIZE, (h + 1) * HEAD_SIZE)
            part = q[s, :, at].astype(F32)
            turned = part * cosine + pltpu.roll(part, HEAD_SIZE // 2, 1) * sine
            qbuf[s, 0, 0, :, at] = turned.astype(BF16)
    for copy in local[2:5]:
        copy.wait()
    gb[tp] = gain[...].astype(F32).reshape(1, W)
    wanted = column_table(targets)
    for s in range(S):
        tt[s] = jnp.broadcast_to(wanted[:R, s : s + 1], (R, 128))
    pl.semaphore_wait(barrier, len(peers))

    scale = math.log2(math.e) / math.sqrt(HEAD_SIZE)
    group = Y * R

    def attend(members, s):
        logs = [{} for _ in members]
        for h in range(heads):
            at = slice(h * HEAD_SIZE, (h + 1) * HEAD_SIZE)
            block = [qbuf[s, e, :, :, at].reshape(group, HEAD_SIZE) for e in members]
            scores = lax.dot_general(
                jnp.concatenate(block, axis=0),
                keys[s, :, at],
                (((1,), (1,)), ((), ())),
                preferred_element_type=F32,
            )
            top = jnp.max(scores, -1, keepdims=True)
            weights = jnp.exp2((scores - top) * scale)
            total = jnp.sum(weights, -1, keepdims=True)
            summed = jnp.dot(
                weights.astype(BF16), values[s, :, at], preferred_element_type=F32
            )
            summed = (summed / total).astype(BF16)
            log_sum = top * (1.0 / math.sqrt(HEAD_SIZE)) + jnp.log(total)
            for place, e in enumerate(members):
                rows = slice(place * group, (place + 1) * group)
                obuf[e, s, :, at] = summed[rows]
                logs[place][h] = log_sum[rows]
        for place, e in enumerate(members):
            ostat[e, s] = columns_to_tile(logs[place])[:heads]

    def attend_first():
        attend([0], 0)

    sides = {1: [], 2: [1]}.get(X, [1, X - 1])
    opposite, y_steps = x_order[len(sides) :], [0] + y_order
    sent_y, sent_x = {}, {}
    for s in range(S):
        for d in y_order:
            sent_y[s, d] = send(qbuf.at[s, 0, 0], qbuf.at[s, 0, d], on_y(d))
    sent_gains = {d: send(gb.at[tp], gb.at[tp], on_tp(d)) for d in range(1, 2 * Z)}
    sent_head = {j: send(wh.at[:, 0:128], wh.at[:, j * 128 : (j + 1) * 128], on_pair(j)) for j in (2, 1)}

    def queries_on(s, ways, d):
        for e in ways:
            sent_x[s, e, d] = send(qbuf.at[s, 0, d], qbuf.at[s, e, d], on_x(e))

    for s in range(S):
        queries_on(s, sides, 0)
        for at, d in enumerate(y_order):
            recv(sent_y[s, d], qbuf.at[s, 0, d])
            queries_on(s, sides, d)
            if at >= 2:
                queries_on(s, opposite, y_steps[at - 2])
        for d in y_steps[max(Y - 3, 0) :]:
            queries_on(s, opposite, d)
        if s == 0:
            for copy in local[5:]:
                copy.wait()
            attend_first()
    y_direct = [d for d in y_order if Y < 8 or min(d, Y - d) <= 2]
    sent_proj = {d: send(wo.at[k, y], wo.at[k, y], on_y(d)) for d in reversed(y_direct)}

    def proj_from(d):
        return wo.at[k, lax.rem(y - d + Y, Y)]

    def half_of(ref, first):
        return ref.at[: W // 2] if first else ref.at[W // 2 :]


    def spread_x(numbers, block, slots, s):
        @pl.when(k == s)
        def _():
            slots[x, k] = block[s]
            for e in x_order:
                copy_of(numbers["same", e], block.at[s], slots.at[x, k], on_x(e)).start()

        @pl.when(k != s)
        def _():
            for e in [0] + x_order:
                there = other_core(on_x(e))
                copy_of(numbers["other", e], block.at[s], slots.at[x, k], there).start()

    def numbers_for(block, slots):
        numbers = {}
        for way, steps in (("same", x_order), ("other", [0] + x_order)):
            for e in steps:
                numbers[way, e] = len(started)
                started.append(copy_of(len(started), block.at[0], slots.at[x, k], on_pair(1)))
        return numbers

    def gathered_x(numbers, slots):
        for (way, e), number in numbers.items():
            recv(number, slots.at[lax.rem(x - e + X, X), k if way == "same" else 1 - k])

    sent_resid = numbers_for(resid, rb)
    for s in range(S):
        spread_x(sent_resid, resid, rb, s)

    sent_o, sent_s = {}, {}

    def attend_others(members, s):
        for e in members:
            for d in y_steps:
                recv(sent_x[s, e, d], qbuf.at[s, e, d])
        if members:
            attend(members, s)
        for e in members:
            sent_o[e, s] = send(obuf.at[e, s], xr.at[e, s], on_x(-e))
            sent_s[e, s] = send(ostat.at[e, s], xs.at[e, s], on_x(-e))

    attend([0], 1)
    for s in range(S):
        attend_others(sides, s)
        attend_others(opposite, s)

    for d in y_direct:
        recv(sent_proj[d], proj_from(d))
    if Y == 8:
        for step, d in ((1, 2), (-1, Y - 2)):
            sent_proj[d + step] = send(proj_from(d), proj_from(d), on_y(step))
        for step, d in ((2, 2), (-2, Y - 2)):
            part = (step > 0, Y // 2)
            sent_proj[part] = send(*[half_of(proj_from(d), step > 0)] * 2, on_y(step))

    sent_yo, sent_ys = {}, {}
    for s in range(S):
        for e in x_order:
            recv(sent_o[e, s], xr.at[e, s])
            recv(sent_s[e, s], xs.at[e, s])
        shares, ystat[s] = merge([ostat[0, s]] + [xs[e, s] for e in x_order])
        table = transposed(shares)
        for h in range(heads):
            at = slice(h * HEAD_SIZE, (h + 1) * HEAD_SIZE)
            total = None
            for place, e in enumerate([0] + x_order):
                column = place * heads + h
                part = obuf[0, s, :, at] if e == 0 else xr[e, s, :, at]
                part = part.astype(F32) * table[:group, column : column + 1]
                total = part if total is None else total + part
            yb[s, :, :, at] = total.reshape(Y, R, HEAD_SIZE).astype(BF16)
        for d in y_order:
            sent_yo[d, s] = send(yb.at[s, d], yr.at[s, d], on_y(-d))
            sent_ys[d, s] = send(ystat.at[s], ys.at[s, d], on_y(-d))
    if Y == 8:
        for d in (3, Y - 3):
            recv(sent_proj[d], proj_from(d))
        for first in (True, False):
            recv(sent_proj[first, Y // 2], half_of(proj_from(Y // 2), first))
    sent_proj = send(wo.at[k], wo.at[k], on_pair(1))
    sent_rows = numbers_for(ab, at_x)
    for s in range(S):
        for d in y_order:
            recv(sent_yo[d, s], yr.at[s, d])
            recv(sent_ys[d, s], ys.at[s, d])
        shares, _ = merge([ystat[s]] + [pltpu.roll(ys[s, d], 128 - d * R, 1) for d in y_order])
        table = transposed(shares)
        for h in range(heads):
            at = slice(h * HEAD_SIZE, (h + 1) * HEAD_SIZE)
            total = None
            for place, d in enumerate([0] + y_order):
                column = place * heads + h
                part = yb[s, 0, :, at] if d == 0 else yr[s, d, :, at]
                part = part.astype(F32) * table[:R, column : column + 1]
                total = part if total is None else total + part
            ab[s, :, at] = total.astype(BF16)
        spread_x(sent_rows, ab, at_x, s)

    recv(sent_proj, wo.at[1 - k])
    gathered_x(sent_resid, rb)
    gathered_x(sent_rows, at_x)
    eight, half = R // 2, cols // 2
    attended = jnp.concatenate([at_x[:, c].reshape(X * R, W) for c in range(2)], axis=1)
    width = wo.shape[-1]
    for j in range(cols // W):
        weights = []
        for c in range(2):
            if width < W:
                each = W // width
                weights.append(
                    jnp.concatenate([wo[c, j * each + i] for i in range(each)], axis=1)
                )
            else:
                first = j * W
                weights.append(wo[c, first // width, :, first % width : first % width + W])
        part = jnp.dot(attended, jnp.concatenate(weights, axis=0), preferred_element_type=F32)
        block = x * (cols // W) + j
        mine = (z == block // 2).astype(F32)
        part = part + rb[:, j % 2].reshape(X * R, W).astype(F32) * mine
        own[:, :, j * W : (j + 1) * W] = part.reshape(Z, eight, W)

    summed = own[...]
    zs[...] = jnp.concatenate([summed[:, :, :half], summed[:, :, half:]], axis=1).astype(BF16)
    sent = {d: send(zs.at[lax.rem(z + d, Z)], zr.at[d], on_z(d)) for d in z_order}
    for d in range(1, 2 * Z):
        recv(sent_gains[d], gb.at[lax.rem(tp - d + 2 * Z, 2 * Z)])
    stream = own[z]
    for d in z_order:
        recv(sent[d], zr.at[d])
        both = zr[d].astype(F32)
        stream = stream + jnp.concatenate([both[:eight], both[eight:]], axis=1)
    gains = [gb[x * (cols // W) + j] for j in range(cols // W)]
    scaled = stream * jnp.concatenate(gains, axis=1)
    ex[x, y, zh] = jnp.concatenate([scaled[:, :half], scaled[:, half:]], axis=0).astype(BF16)

    def near(e):
        return lax.rem(zh - e + ZH, ZH)

    def piece(i, d, e):
        return ex.at[lax.rem(x - i + X, X), lax.rem(y - d + Y, Y), near(e)]

    z_steps = [0] + zh_order
    x_first = z_steps[-1]
    under_way, busy = [], {}

    opposite_numbers = {}

    def launch_opposite(core, now, step, i, d, e):
        if (d, e) not in opposite_numbers:
            opposite_numbers[d, e] = len(started)
            started.append(copy_of(len(started), piece(i, d, e), piece(i, d, e), on_x(step)))

        @pl.when(k == core)
        def _():
            copy_of(opposite_numbers[d, e], piece(i, d, e), piece(i, d, e), on_x(step)).start()

        if core == 1:
            number = opposite_numbers[d, e]
            heapq.heappush(under_way, (now + 2.5, number, (2, d, e)))

    def launch(now, axis, step, i, d, e):
        size = {"x": X, "y": Y, "z": ZH}[axis]
        device = {"x": on_x, "y": on_y, "z": lambda n: on_z(2 * n)}[axis](step)
        number = send(piece(i, d, e), piece(i, d, e), device)
        way = step % size
        way = way if 2 * way <= size else way - size
        link = (axis, way > 0)
        busy[link] = max(now, busy.get(link, 0.0)) + 0.42 * abs(way)
        there = [i, d, e]
        at = "xyz".index(axis)
        there[at] = (there[at] + step) % size
        hops = abs(way) * (2 if axis == "z" else 1)
        heapq.heappush(under_way, (busy[link] + 2.0 + 0.7 * hops, number, tuple(there)))

    def spread_y(now, i, d, e):
        if d == 0:
            for step in y_direct:
                launch(now, "y", step, i, d, e)
        elif Y == 8 and d in (2, Y - 2):
            step = 1 if d == 2 else -1
            launch(now, "y", step, i, d, e)
            if (i + e + (step > 0)) % 2:
                launch(now, "y", 2 * step, i, d, e)

    def arrived(now, i, d, e):
        if e == x_first and i == d == 0:
            for step in x_order:
                launch(now, "x", step, i, d, e)
        elif e != x_first and i == 0:
            for step in sides:
                launch(now, "x", step, i, d, e)
            if X == 4 and Y == 8 and d not in [0] + y_direct:
                launch_opposite(0, now, 2, i, d, e)
        if e == x_first or i == 0:
            spread_y(now, i, d, e)
        elif X == 4 and i == (1 if (z_steps.index(e) + d) % 2 else X - 1):
            if d in [0] + y_direct:
                launch(now, "x", 1 if i == 1 else -1, i, d, e)
            else:
                launch_opposite(1, now, 1 if i == 1 else -1, i, d, e)

    for e in zh_order:
        launch(0.0, "z", e, 0, 0, 0)
    arrived(0.0, 0, 0, 0)
    lane = lax.broadcasted_iota(jnp.int32, (eight, 128), 1)
    squares = jnp.sum(stream * stream, -1, keepdims=True)
    wanted = tt[k, pl.ds(pl.multiple_of(parity * eight, eight), eight), :] * (x == zh).astype(F32)
    ea[zh] = jnp.where(lane == 0, squares, jnp.where(lane == 1, wanted, 0.0))
    sent_az = {e: send(ea.at[zh], ea.at[zh], on_z(2 * e)) for e in zh_order}
    recv(sent_head[2], wh.at[:, 256:384])
    sent_head[3] = send(wh.at[:, 256:384], wh.at[:, 384:512], on_pair(1))

    block = ZH * eight
    per_tile = 128 // block
    tiles = xa.shape[1]
    sent_ay, sent_ax = {}, {}

    def rows_along_y():
        for e in zh_order:
            recv(sent_az[e], ea.at[near(e)])
        ya[y] = transposed([ea[i] for i in range(ZH)])[:8]
        for d in y_order:
            sent_ay[d] = send(ya.at[y], ya.at[y], on_y(d))

    def rows_along_x():
        for d in y_order:
            recv(sent_ay[d], ya.at[lax.rem(y - d + Y, Y)])
        for i in range(tiles):
            total = None
            for place in range(min(per_tile, Y)):
                tile = ya[i * per_tile + place]
                if place:
                    tile = pltpu.roll(tile, place * block, 1)
                total = tile if total is None else total + tile
            xa[x, i] = total
        for e in x_order:
            sent_ax[e] = send(xa.at[x], xa.at[x], on_x(e))

    slots = Y * ZH * eight

    def multiply(i, e):
        if not complete:
            for j in (1, 3):
                recv(sent_head[j], wh.at[:, j * 128 : (j + 1) * 128])
        from_x, from_z = lax.rem(x - i + X, X), near(e)
        block = ex[from_x, :, from_z].reshape(Y * R, half)
        total = None
        for upper in range(2):
            start = pl.multiple_of(from_x * cols + upper * half, half)
            part = jnp.dot(block, wh[pl.ds(start, half), :], preferred_element_type=F32)
            part = part.reshape(Y, 2, eight, 4 * 128)[:, upper]
            total = part if total is None else total + part
        if e in complete:
            lg[:, from_z] += total
        else:
            lg[:, from_z] = total
        complete.append(e)

    complete = []
    missing = {(i, e): Y for i in range(X) for e in z_steps}
    missing[0, 0] -= 1
    later = [(6.0, rows_along_y), (11.0, rows_along_x)]
    while under_way:
        now, number, place = heapq.heappop(under_way)
        while later and later[0][0] < now:
            later.pop(0)[1]()
        recv(number, piece(*place))
        arrived(now, *place)
        i, _, e = place
        missing[i, e] -= 1
        if missing[i, e] == 0:
            multiply(i, e)
    for _, step in later:
        step()
    if Y == 1:
        multiply(0, 0)
    for e in x_order:
        recv(sent_ax[e], xa.at[lax.rem(x - e + X, X)])
    span = min(128, slots)
    fin = None
    for i in range(tiles):
        total = xa[0, i]
        for from_x in range(1, X):
            total = total + xa[from_x, i]
        table = transposed([lax.rsqrt(total * (1.0 / (X * cols)) + NORM_EPSILON), total])
        logits = lg[i * per_tile : (i + 1) * per_tile].reshape(span, 4 * 128) * table[:span, 0:1]
        wanted = table[:span, 9:10]
        top = jnp.max(logits, -1, keepdims=True)
        sums = jnp.sum(jnp.exp(logits - top), -1, keepdims=True)
        lane = lax.broadcasted_iota(jnp.int32, (span, 128), 1)
        picked = jnp.zeros((span, 128), F32)
        for j in range(4):
            first = (ctx * (2 * Z) + on_pair(j)[1]) * 128
            hit = (lane + first).astype(F32) == wanted
            picked = picked + jnp.where(hit, logits[:, j * 128 : (j + 1) * 128], 0.0)
        tile = columns_to_tile(
            {i: top + jnp.log(sums), 2 + i: jnp.sum(picked, -1, keepdims=True)}
        )
        fin = tile if fin is None else fin + tile
    ft[tp] = fin[:4]

    row = lax.broadcasted_iota(jnp.int32, (8, 128), 0)

    def combine(parts):
        _, log_sum = merge(parts)
        logs = lax.broadcasted_iota(jnp.int32, parts[0].shape, 0) < parts[0].shape[0] // 2
        return jnp.where(logs, log_sum, functools.reduce(jnp.add, parts))

    sent = {d: send(ft.at[tp], ft.at[tp], on_tp(d)) for d in range(1, 2 * Z)}
    settled = len(started)
    for copy in started:
        copy.wait_send()
    for d in range(1, 2 * Z):
        recv(sent[d], ft.at[lax.rem(tp - d + 2 * Z, 2 * Z)])
    for s in range(S):
        first, second = (
            combine([ft[4 * i + 2 * upper + s] for i in range(ZH)]) for upper in range(2)
        )
        fy[y, s] = jnp.concatenate([first[:2], second[:2], first[2:], second[2:]], axis=0)
    sent = {d: send(fy.at[y], fy.at[y], on_y(d)) for d in y_order}
    for d in y_order:
        recv(sent[d], fy.at[lax.rem(y - d + Y, Y)])
    for s in range(S):
        fx[x, s] = combine([fy[i, s] for i in range(Y)])
    sent = {e: send(fx.at[x], fx.at[x], on_x(e)) for e in x_order}
    for e in x_order:
        recv(sent[e], fx.at[lax.rem(x - e + X, X)])

    lane = lax.broadcasted_iota(jnp.int32, (8, 128), 1)
    from_y = lax.rem(row, 2) * per_tile + lane // block
    from_x = lax.rem(lane, block) // eight
    slot = (from_x * Y + from_y) * R + (row // 2) * eight + lax.rem(lane, eight)
    counted = (row < 4) & (from_y < Y)
    sample_sum, tokens = None, []
    first = lax.rem(y, per_tile) * block + x * eight
    member = lax.broadcasted_iota(jnp.int32, (R, 128), 0)
    place = lax.broadcasted_iota(jnp.int32, (R, 128), 1) == first + lax.rem(member, eight)
    for s in range(S):
        tile = combine([fx[i, s] for i in range(X)])
        tile = tile - pltpu.roll(tile, 4, 0)
        tile = jnp.where(counted & (slot < live_rows[s]), tile, 0.0)
        total = jnp.sum(jnp.sum(tile, 1, keepdims=True), 0, keepdims=True)
        total = total / jnp.full((1, 1), mask_total[s], jnp.int32).astype(F32)
        sample_sum = total if sample_sum is None else sample_sum + total
        in_first = y < per_tile
        lower = jnp.where(in_first, tile[0:1], tile[1:2])
        upper = jnp.where(in_first, tile[2:3], tile[3:4])
        tokens.append(jnp.where(place, jnp.where(member < eight, lower, upper), 0.0))
    loss[...] = sample_sum * (1.0 / S)
    token = jnp.sum(transposed(tokens), 0, keepdims=True)
    for s in range(S):
        out[0, s : s + 1, :] = token[:, s * R : (s + 1) * R]
    finished = [
        pltpu.make_async_copy(out, out_hbm, local_sem.at[0]),
        pltpu.make_async_copy(loss, loss_hbm, local_sem.at[1]),
    ]
    for copy in finished:
        copy.start()
    for copy in started[settled:]:
        copy.wait_send()
    for copy in finished:
        copy.wait()
    assert len(started) == copies(X, Y, Z), len(started)


def copies(X, Y, Z):
    x, y, z, zh = X - 1, Y - 1, Z - 1, Z // 2 - 1
    count = 2 * (y + x + x * y) + 2 + 2 * Z - 1 + (8 if Y == 8 else y) + 2 * (2 * x + 1) + 4 * x + 4 * y + 1 + z
    count += X * Y * Z // 2 - 1 + 1 + zh + y + x
    return count + 2 * Z - 1 + y + x


def on_device(
    sizes,
    queries,
    positions,
    cached_keys,
    cached_values,
    residual_rows,
    out_proj,
    norm_gain,
    head_weight,
    targets,
    live_rows,
    mask_total,
):
    X, Y, Z = sizes
    S, R, W = queries.shape
    L = cached_keys.shape[1]
    D = head_weight.shape[0]
    cols = D // X
    ZH = Z // 2
    block = ZH * (R // 2)
    tiles = -(-Y * block // 128)
    hbm = pl.BlockSpec(memory_space=pl.ANY)
    scratch = [
        ((S, R, W), BF16),
        ((S, R), jnp.int32),
        ((S, R), jnp.int32),
        ((S, R, W), BF16),
        ((W,), BF16),
        ((S, L, W), BF16),
        ((S, L, W), BF16),
        ((S, X, Y, R, W), BF16),
        ((X, S, Y * R, W), BF16),
        ((X, S, W // HEAD_SIZE, 128), F32),
        ((X, S, Y * R, W), BF16),
        ((X, S, W // HEAD_SIZE, 128), F32),
        ((S, Y, R, W), BF16),
        ((S, W // HEAD_SIZE, 128), F32),
        ((S, Y, R, W), BF16),
        ((S, Y, W // HEAD_SIZE, 128), F32),
        ((S, R, W), BF16),
        ((X, 2, R, W), BF16),
        ((X, 2, R, W), BF16),
        ((2 * Z, 1, W), F32),
        ((2, Y, W, out_proj.shape[1]), BF16),
        ((D, 4 * 128), BF16),
        ((Z, R // 2, cols), F32),
        ((S, R, 128), F32),
        ((Z, R, cols // 2), BF16),
        ((Z, R, cols // 2), BF16),
        ((ZH, R // 2, 128), F32),
        ((X, Y, ZH, R, cols // 2), BF16),
        ((Y, 8, 128), F32),
        ((X, tiles, 8, 128), F32),
        ((Y, ZH, R // 2, 4 * 128), F32),
        ((2 * Z, 4, 128), F32),
        ((Y, S, 8, 128), F32),
        ((X, S, 8, 128), F32),
        ((1, S, R), F32),
        ((1, 1), F32),
    ]
    count = copies(X, Y, Z)
    token_nll, loss = pl.pallas_call(
        functools.partial(kernel, sizes),
        out_shape=[jax.ShapeDtypeStruct((1, S, R), F32), jax.ShapeDtypeStruct((1, 1), F32)],
        in_specs=[hbm] * 11,
        out_specs=[hbm, hbm],
        scratch_shapes=[pltpu.SMEM((S,), jnp.int32)] * 2
        + [pltpu.VMEM(*shape) for shape in scratch]
        + [
            pltpu.SemaphoreType.DMA((11,)),
            pltpu.SemaphoreType.DMA((count,)),
            pltpu.SemaphoreType.DMA((count,)),
        ],
        compiler_params=pltpu.CompilerParams(
            collective_id=0, has_side_effects=True, vmem_limit_bytes=60 * 1024 * 1024
        ),
        name="cloze",
    )(
        live_rows, mask_total, queries, positions, targets, residual_rows,
        norm_gain, cached_keys, cached_values, out_proj, head_weight,
    )
    return (token_nll.reshape(S, R), loss.reshape(()))


def solution(mesh):
    Z = mesh.shape["tp"] // 2
    X = Z // 2
    sizes = (X, mesh.shape["ctx"] // X, Z)
    in_specs = (
        P(None, "ctx", "tp"),
        P(None, "ctx"),
        P(None, "ctx", "tp"),
        P(None, "ctx", "tp"),
        P(None, "ctx", "tp"),
        P("tp", "ctx"),
        P("tp"),
        P(None, ("ctx", "tp")),
        P(None, "ctx"),
        P(),
        P(),
    )
    return jax.shard_map(
        functools.partial(on_device, sizes),
        mesh=mesh,
        in_specs=in_specs,
        out_specs=(P(None, "ctx"), P()),
        check_vma=False,
    )
```
